32 devices in a mesh: src: 4 (over y, core), tile: 8 (over z, x).
Axes of the slice: x: 2, y: 2, z: 4, core: 2. Of those that a mesh axis runs over, the one named last changes fastest.
Arguments:
- mask: bfloat16 [256, 4096], P('src', 'tile'), may hold values from -6 to 6
- target: bfloat16 [256, 4096], P('src', 'tile'), may hold values from 0 to 1
- start_block: float32 [2, 24, 128, 128], replicated, may hold values from -6 to 6
- zernike: float32 [8, 37], replicated, may hold values from -0.3 to 0.3
- source_points: int32 [512, 2], replicated, may hold values from -24 to 24
- source_weight: float32 [512], replicated, may hold values from 0.25 to 1
- tile_slit: int32 [16], P('tile'), may hold values from 0 to 7
Outputs:
- resist: bfloat16 [256, 4096], P('src', 'tile')
- mask_grad: bfloat16 [256, 4096], P('src', 'tile')
The draws below stay inside these ranges and needn't reach their ends.
All inputs are finite; a program needn't handle non-finite values.
Results may differ from the reference program's by a relative error of at most 0.024.
Values may be sent and summed in bfloat16 or wider, within the bound.
A program may use at most 128 MiB of HBM per device.

```python
import math
import jax
import jax.numpy as jnp
from jax import lax

KB = 128
NR = 24
NZ = 37
SOURCE = 512
RAD = 40
SHIFT = 24
HALO = 64
ITERS = 4
TS = 256
TILES = 16
SLITS = 8


def draw_tile_slit(key, part):
    key_values, key_places = jax.random.split(key)
    values = jax.random.randint(key_values, (TILES,), 0, SLITS, dtype=jnp.int32)
    places = jax.random.permutation(key_places, TILES)
    values = values.at[places[0]].set(0)
    values = values.at[places[1]].set(SLITS - 1)
    return values


def touch_ends(values, key, smallest, top_value):
    longest = values.shape.index(max(values.shape))
    spots = []
    for shift in (0, 1):
        where = [jax.random.randint(jax.random.fold_in(key, axis), (), 0, length) for axis, length in enumerate(values.shape)]
        where[longest] = (where[longest] + shift) % values.shape[longest]
        spots.append(tuple(where))
    return values.at[spots[0]].set(smallest).at[spots[1]].set(top_value)


def steps_of(own_key, shape, cuts, low, largest):
    gain = 1.0
    for dim, blocks in cuts:
        draws = jax.random.uniform(jax.random.fold_in(jax.random.fold_in(own_key, 6), dim), (blocks,), jnp.float32, low / len(cuts), largest / len(cuts))
        gain = gain * jnp.repeat(jnp.exp(draws), shape[dim] // blocks).reshape((-1,) + (1,) * (len(shape) - 1 - dim))
    return gain


def bell_draw(rng, shape, width, most, cuts=(), held_as=jnp.bfloat16):
    array = jax.random.normal(rng, shape, jnp.float32) * width
    if len(cuts) > 0:
        array = steps_of(rng, shape, cuts, -0.22, 0.18) * array
    return jnp.clip(array, min=-most, max=most).astype(held_as)


def setup_inputs(seed: int = 0) -> dict:
    splits = jax.random.split(jax.random.key(seed), 8)
    return {
        "mask": bell_draw(splits[0], (TS, TILES * TS), 1.0, 6.0, ((0, 4), (1, 8))),
        "target": jnp.clip(1.0 * jax.random.uniform(splits[1], (TS, TILES * TS), jnp.float32) ** steps_of(splits[1], (TS, TILES * TS), ((0, 4), (1, 8)), -0.2, 0.2), 0.0, 1.0).astype(jnp.bfloat16),
        "start_block": bell_draw(splits[2], (2, NR, KB, KB), 1.0, 6.0, (), jnp.float32),
        "zernike": bell_draw(splits[3], (SLITS, NZ), 0.05, 0.3, (), jnp.float32),
        "source_points": touch_ends(jax.random.randint(splits[4], (SOURCE, 2), -SHIFT, SHIFT + 1), jax.random.fold_in(splits[4], 1), -SHIFT, SHIFT).astype(jnp.int32),
        "source_weight": jnp.clip(jnp.exp(jax.random.uniform(splits[5], (SOURCE,), jnp.float32, math.log(0.25), math.log(1.0))), 0.25, 1.0),
        "tile_slit": draw_tile_slit(jax.random.fold_in(splits[7], 71), 0),
    }


STEEPNESS = 4.0
THRESHOLD = 0.5
RIDGE_SHARE = 0.001
EXACT_MODE = lax.Precision.HIGHEST

def noll_terms(term_count):
    listing = []
    degree = 0
    while len(listing) < term_count:
        for azimuth in range(degree % 2, degree + 1, 2):
            if azimuth == 0:
                listing.append((degree, 0, 0))
            else:
                for repeat in range(2):
                    number = len(listing) + 1
                    listing.append((degree, azimuth, 2 if number % 2 == 0 else 1))
        degree += 1
    return listing[:term_count]

def radial_terms(degree, azimuth):
    powers = []
    for counter in range((degree - azimuth) // 2 + 1):
        factor = (-1) ** counter * math.factorial(degree - counter) / (math.factorial(counter) * math.factorial((degree + azimuth) // 2 - counter) * math.factorial((degree - azimuth) // 2 - counter))
        powers.append((degree - 2 * counter, factor))
    return powers

def pupil_grid(coefficients):
    extent = KB + 2 * SHIFT
    coords = jnp.arange(extent, dtype=jnp.int32) - (KB // 2 + SHIFT)
    row_coord = coords[:, None]
    col_coord = coords[None, :]
    radius_sq = row_coord * row_coord + col_coord * col_coord
    inside = (radius_sq <= RAD * RAD).astype(jnp.float32)
    radius = jnp.sqrt(radius_sq.astype(jnp.float32)) / RAD
    azimuth_angle = jnp.arctan2(col_coord.astype(jnp.float32) + 0.0 * radius, row_coord.astype(jnp.float32) + 0.0 * radius)
    aberration = jnp.zeros((extent, extent), jnp.float32)
    for position, (degree, azimuth, parity) in enumerate(noll_terms(NZ)):
        radial = jnp.zeros((extent, extent), jnp.float32)
        for exponent, factor in radial_terms(degree, azimuth):
            radial = radial + factor * radius ** exponent
        if azimuth == 0:
            profile = math.sqrt(degree + 1.0) * radial
        elif parity == 2:
            profile = math.sqrt(2.0 * degree + 2.0) * radial * jnp.cos(azimuth * azimuth_angle)
        else:
            profile = math.sqrt(2.0 * degree + 2.0) * radial * jnp.sin(azimuth * azimuth_angle)
        aberration = aberration + coefficients[position] * profile
    phase_angle = 2.0 * math.pi * aberration
    return jnp.stack([inside * jnp.cos(phase_angle), inside * jnp.sin(phase_angle)])

def source_windows(pupil_values, offsets, row_start, row_total):

    def single(offset):
        return lax.dynamic_slice(pupil_values, (jnp.zeros((), jnp.int32), (offset[0] + SHIFT + row_start).astype(jnp.int32), (offset[1] + SHIFT).astype(jnp.int32)), (2, row_total, KB))
    windowed = jax.vmap(single)(offsets)
    return windowed.reshape(offsets.shape[0], 2 * row_total * KB)

def pupil_products(windows, kernel_block):
    real_pairs = jnp.concatenate([kernel_block[0], kernel_block[1]], axis=1)
    imag_pairs = jnp.concatenate([kernel_block[1], -kernel_block[0]], axis=1)
    stacked = jnp.concatenate([real_pairs, imag_pairs], axis=0)
    return jnp.einsum('sf,kf->sk', windows, stacked, precision=EXACT_MODE)

def spread_terms(windows, products):
    spread = jnp.einsum('sk,sf->kf', products, windows, precision=EXACT_MODE)
    half_width = spread.shape[1] // 2
    image_re = spread[:NR, :half_width] - spread[NR:, half_width:]
    image_im = spread[NR:, :half_width] + spread[:NR, half_width:]
    return jnp.stack([image_re, image_im])

def inner_products(left_block, right_block):
    return jnp.einsum('zkf,zlf->kl', left_block, right_block, precision=EXACT_MODE)

def orthonormal(applied, gram_matrix):
    shift_term = RIDGE_SHARE * jnp.trace(gram_matrix) / NR + 1e-06
    factor = jnp.linalg.cholesky(gram_matrix + shift_term * jnp.eye(NR, dtype=jnp.float32))
    inverse = jax.scipy.linalg.solve_triangular(factor, jnp.eye(NR, dtype=jnp.float32), lower=True)
    return jnp.einsum('kl,zlf->zkf', inverse, applied, precision=EXACT_MODE)

def synthesize(coefficients, source_points, source_weight, start_block):
    pupil_values = pupil_grid(coefficients)
    windows = source_windows(pupil_values, source_points, 0, KB)
    weighting = source_weight / (math.pi * RAD * RAD * jnp.sum(source_weight))
    kernel_block = start_block.reshape(2, NR, KB * KB)
    for iteration in range(ITERS + 1):
        products = pupil_products(windows, kernel_block) * weighting[:, None]
        applied = spread_terms(windows, products)
        if iteration < ITERS:
            kernel_block = orthonormal(applied, inner_products(applied, applied))
    mixing = inner_products(kernel_block, applied)
    mixing = (0.5 * (mixing + mixing.T)).astype(jnp.bfloat16)
    return (kernel_block.reshape(2, NR, KB, KB).astype(jnp.bfloat16), mixing)

def phase_table(positions, period):
    frequency = jnp.arange(KB, dtype=jnp.int32) - KB // 2
    residue = jnp.mod(positions[:, None] * frequency[None, :], period)
    angles = 2.0 * math.pi / period * residue.astype(jnp.float32)
    return (jnp.cos(angles).astype(jnp.bfloat16), jnp.sin(angles).astype(jnp.bfloat16))

def row_phase_table(positions):
    cosine_table, sine_table = phase_table(positions, TS)
    return jnp.concatenate([cosine_table, sine_table], axis=1)

def column_tables():
    patch_width = TS + 2 * HALO
    cosine_table, sine_table = phase_table(jnp.arange(patch_width, dtype=jnp.int32), patch_width)
    column_forward = jnp.concatenate([cosine_table, -sine_table], axis=1)
    inner_cos = cosine_table[HALO:HALO + TS]
    inner_sin = sine_table[HALO:HALO + TS]
    column_inverse = jnp.concatenate([inner_cos, -inner_sin], axis=1)
    column_adjoint = jnp.concatenate([inner_cos, inner_sin], axis=1)
    return (column_forward, column_inverse, column_adjoint)

def contract(form, left_array, right_array):
    return jnp.einsum(form, left_array.astype(jnp.float32), right_array.astype(jnp.float32), precision=EXACT_MODE)

def image_tile(patch, goal_tile, kernel, mixing, row_table, column_forward, column_inverse, column_adjoint):
    patch_width = TS + 2 * HALO
    spectrum_scale = 1.0 / math.sqrt(TS * patch_width)
    columns = jnp.dot(patch.astype(jnp.float32), column_forward.astype(jnp.float32), preferred_element_type=jnp.float32).astype(jnp.bfloat16)
    row_sums = contract('xc,xd->cd', row_table, columns)
    spectrum_re = spectrum_scale * (row_sums[:KB, :KB] + row_sums[KB:, KB:])
    spectrum_im = spectrum_scale * (row_sums[:KB, KB:] - row_sums[KB:, :KB])
    kernel_re = kernel[0].astype(jnp.float32)
    kernel_im = kernel[1].astype(jnp.float32)
    product_re = (kernel_re * spectrum_re + kernel_im * spectrum_im).astype(jnp.bfloat16)
    product_im = (kernel_re * spectrum_im - kernel_im * spectrum_re).astype(jnp.bfloat16)
    blocks = jnp.concatenate([jnp.concatenate([product_re, product_im], axis=2), jnp.concatenate([-product_im, product_re], axis=2)], axis=1)
    rows_mixed = contract('xc,kcd->kxd', row_table, blocks).astype(jnp.bfloat16)
    fields = contract('kxc,yc->kxy', rows_mixed, column_inverse)
    mixed_fields = jnp.einsum('kl,lxy->kxy', mixing.astype(jnp.float32), fields, precision=EXACT_MODE)
    intensity = lax.optimization_barrier(jnp.sum(fields * mixed_fields, axis=0))
    resist = jax.nn.sigmoid(STEEPNESS * (intensity - THRESHOLD))
    resist_slope = 2.0 * (resist - goal_tile.astype(jnp.float32)) * STEEPNESS * resist * (1.0 - resist)
    field_grad = (2.0 * mixed_fields * resist_slope[None]).astype(jnp.bfloat16)
    adjoint_cols = contract('kxy,yc->kxc', field_grad, column_adjoint).astype(jnp.bfloat16)
    adjoint_rows = contract('xc,kxd->kcd', row_table, adjoint_cols)
    turned_re = adjoint_rows[:, :KB, :KB] - adjoint_rows[:, KB:, KB:]
    turned_im = adjoint_rows[:, :KB, KB:] + adjoint_rows[:, KB:, :KB]
    grad_re = lax.optimization_barrier(jnp.sum(kernel_re * turned_re + kernel_im * turned_im, axis=0))
    grad_im = lax.optimization_barrier(jnp.sum(kernel_im * turned_re - kernel_re * turned_im, axis=0))
    back_re = (spectrum_scale * grad_re).astype(jnp.bfloat16)
    back_im = (spectrum_scale * grad_im).astype(jnp.bfloat16)
    back_block = jnp.concatenate([jnp.concatenate([back_re, back_im], axis=1), jnp.concatenate([-back_im, back_re], axis=1)], axis=0)
    back_rows = jnp.dot(row_table.astype(jnp.float32), back_block.astype(jnp.float32), preferred_element_type=jnp.float32).astype(jnp.bfloat16)
    patch_grad = contract('xc,yc->xy', back_rows, column_forward)
    return (resist.astype(jnp.bfloat16), patch_grad)

def reference(mask, target, start_block, zernike, source_points, source_weight, tile_slit):

    def per_slit(coefficients):
        return synthesize(coefficients, source_points, source_weight, start_block)
    kernels, mixings = lax.map(per_slit, zernike)
    patch_width = TS + 2 * HALO
    padded = jnp.pad(mask, ((0, 0), (HALO, HALO)))
    row_table = row_phase_table(jnp.arange(TS, dtype=jnp.int32))
    column_forward, column_inverse, column_adjoint = column_tables()

    def per_tile(tile_number):
        start_col = (tile_number * TS).astype(jnp.int32)
        patch = lax.dynamic_slice_in_dim(padded, start_col, patch_width, 1)
        goal_tile = lax.dynamic_slice_in_dim(target, start_col, TS, 1)
        slit_index = tile_slit[tile_number]
        return image_tile(patch, goal_tile, kernels[slit_index], mixings[slit_index], row_table, column_forward, column_inverse, column_adjoint)
    resist_tiles, patch_grads = lax.map(per_tile, jnp.arange(TILES, dtype=jnp.int32))
    inner_part = patch_grads[:, :, HALO:HALO + TS]
    low_rims = patch_grads[:, :, :HALO]
    high_rims = patch_grads[:, :, TS + HALO:]
    empty_rim = jnp.zeros((1, TS, HALO), jnp.float32)
    from_left = jnp.concatenate([empty_rim, high_rims[:-1]], axis=0)
    from_right = jnp.concatenate([low_rims[1:], empty_rim], axis=0)
    total = inner_part + jnp.pad(from_left, ((0, 0), (0, 0), (0, TS - HALO))) + jnp.pad(from_right, ((0, 0), (0, 0), (TS - HALO, 0)))
    resist = jnp.transpose(resist_tiles, (1, 0, 2)).reshape(TS, TILES * TS)
    mask_grad = jnp.transpose(total, (1, 0, 2)).reshape(TS, TILES * TS).astype(jnp.bfloat16)
    return (resist, mask_grad)
```

```python
import functools
import math

import jax
import jax.numpy as jnp
import ml_dtypes
import numpy as np
from jax import lax
from jax.experimental import pallas as pl
from jax.experimental.pallas import tpu as pltpu
from jax.sharding import PartitionSpec as P

KB = 128
NR = 24
NZ = 37
RAD = 40
SHIFT = 24
HALO = 64
ITERS = 4
TS = 256
LAGS = 2 * SHIFT + 1
LP = 64
DISC = 88

STEEPNESS = 4.0
THRESHOLD = 0.5
RIDGE_SHARE = 0.001
F32 = jnp.float32
BF16 = jnp.bfloat16


def with_halo(cells, sides, width):
    for axis, dim in sides:
        count = lax.axis_size(axis)
        ends = count - 1
        head = lax.slice_in_dim(cells, 0, width, axis=dim)
        tail = lax.slice_in_dim(cells, cells.shape[dim] - width, cells.shape[dim], axis=dim)
        cells = jnp.concatenate(
            [
                lax.ppermute(tail, axis, [(i, (i + 1) % count) for i in range(ends)]),
                cells,
                lax.ppermute(head, axis, [((i + 1) % count, i) for i in range(ends)]),
            ],
            axis=dim,
        )
    return cells


def noll_terms(term_count):
    listing = []
    degree = 0
    while len(listing) < term_count:
        for azimuth in range(degree % 2, degree + 1, 2):
            if azimuth == 0:
                listing.append((degree, 0, 0))
            else:
                for repeat in range(2):
                    number = len(listing) + 1
                    listing.append((degree, azimuth, 2 if number % 2 == 0 else 1))
        degree += 1
    return listing[:term_count]


def radial_terms(degree, azimuth):
    powers = []
    for counter in range((degree - azimuth) // 2 + 1):
        factor = (
            (-1) ** counter
            * math.factorial(degree - counter)
            / (
                math.factorial(counter)
                * math.factorial((degree + azimuth) // 2 - counter)
                * math.factorial((degree - azimuth) // 2 - counter)
            )
        )
        powers.append((degree - 2 * counter, factor))
    return powers


@functools.lru_cache(None)
def zernike_table():
    u = (np.arange(DISC) - RAD)[:, None]
    v = (np.arange(KB) - RAD)[None, :]
    inside = (u * u + v * v <= RAD * RAD).astype(np.float64)
    rho = np.sqrt(u * u + v * v) / RAD
    theta = np.arctan2(v + 0.0 * u, u + 0.0 * v)
    planes = []
    for degree, azimuth, parity in noll_terms(NZ):
        radial = sum(f * rho**e for e, f in radial_terms(degree, azimuth))
        if azimuth == 0:
            plane = math.sqrt(degree + 1.0) * radial
        else:
            turn = np.cos if parity == 2 else np.sin
            plane = math.sqrt(2.0 * degree + 2.0) * radial * turn(azimuth * theta)
        planes.append(plane * inside)
    planes.append(inside)
    return np.stack(planes).astype(np.float32)


def split_table(table, axis):
    high = table.astype(ml_dtypes.bfloat16)
    low = (table - high.astype(np.float64)).astype(ml_dtypes.bfloat16)
    return np.concatenate([high, high, low], axis=axis)


@functools.lru_cache(None)
def dft_tables():
    f = np.arange(KB)
    angle = 2.0 * np.pi / KB * ((f[:, None] * f[None, :]) % KB)
    c, s = np.cos(angle), np.sin(angle)
    keep = np.arange(LP) < LAGS
    cy, sy = c[:LP] * keep[:, None], s[:LP] * keep[:, None]
    scale = 1.0 / (KB * KB)
    full = np.block([[c, -s], [s, c]])
    lag = np.block([[cy, -sy], [sy, cy]])
    inv_lag = np.block([[cy.T, sy.T], [-sy.T, cy.T]]) * scale
    inv_full = np.block([[c, s], [-s, c]]) * scale
    left_full = np.concatenate([c, s], axis=0)
    left_lag = np.concatenate([cy.T, sy.T], axis=0)
    left_inv = np.concatenate([cy, sy], axis=0)
    return (
        split_table(full, 0),
        split_table(lag, 0),
        split_table(inv_lag, 0),
        split_table(inv_full, 0),
        split_table(left_full, 1),
        split_table(left_lag, 1),
        split_table(left_inv, 1),
    )


def halves(x):
    high = x.astype(BF16)
    return high, (x - high.astype(F32)).astype(BF16)


def right_mul(x, table, passes):
    if passes == 1:
        return jnp.dot(x.astype(BF16), table[: x.shape[1]], preferred_element_type=F32)
    high, low = halves(x)
    return jnp.dot(
        jnp.concatenate([high, low, high], axis=1), table, preferred_element_type=F32
    )


def left_mul(table, x, passes):
    if passes == 1:
        return jnp.dot(table[:, : x.shape[0]], x.astype(BF16), preferred_element_type=F32)
    high, low = halves(x)
    return jnp.dot(
        table, jnp.concatenate([high, low, high], axis=0), preferred_element_type=F32
    )


def nt_mul(x, y):
    xh, xl = halves(x)
    yh, yl = halves(y)
    dims = (((1,), (1,)), ((), ()))
    return (
        lax.dot_general(xh, yh, dims, preferred_element_type=F32)
        + lax.dot_general(xl, yh, dims, preferred_element_type=F32)
        + lax.dot_general(xh, yl, dims, preferred_element_type=F32)
    )


def small_mul(m, x):
    mh, ml = halves(m)
    xh, xl = halves(x)
    return (
        jnp.dot(mh, xh, preferred_element_type=F32)
        + jnp.dot(ml, xh, preferred_element_type=F32)
        + jnp.dot(mh, xl, preferred_element_type=F32)
    )


def forward_turn(t):
    n = t.shape[0] // 2
    return t[:n, :KB] + t[n:, KB:], t[:n, KB:] - t[n:, :KB]


def inverse_turn(t):
    n = t.shape[0] // 2
    return jnp.concatenate([t[:n, :KB] - t[n:, KB:], t[:n, KB:] + t[n:, :KB]], axis=1)


def eliminate(gram, floor):
    row = lax.broadcasted_iota(jnp.int32, (NR, KB), 0)
    lane = lax.broadcasted_iota(jnp.int32, (NR, KB), 1)
    aug = jnp.concatenate([gram, jnp.zeros((NR, KB - NR), F32)], axis=1)
    aug = aug + jnp.where(lane == row + NR, 1.0, 0.0)
    rowid = lax.broadcasted_iota(jnp.int32, (NR, 1), 0)
    scales = jnp.zeros((NR, 1), F32)
    for j in range(NR):
        pivot_row = aug[j : j + 1, :]
        pivot = pivot_row[:, j : j + 1]
        good = pivot > floor
        safe = jnp.where(good, pivot, 1.0)
        inverse = jnp.where(good, 1.0 / safe, 0.0)
        root = jnp.where(good, lax.rsqrt(safe), 0.0)
        factor = jnp.where(rowid > j, aug[:, j : j + 1] * inverse, 0.0)
        aug = aug - factor * pivot_row
        scales = jnp.where(rowid == j, root, scales)
    return aug * scales


def synth_kernel(
    slit_ref, zern_ref, basis_ref, block_ref, points_ref, weight_ref,
    full, lag, inv_lag, inv_full, left_full, left_lag, left_inv,
    out_ref, y_ref, z_ref, s_ref, u_ref, pre_ref, pim_ref, *, gpasses,
):
    lane2 = lax.broadcasted_iota(jnp.int32, (1, KB), 1)
    slit = slit_ref[0]
    waves = zern_ref[slit, 0] * basis_ref[0]
    for z in range(1, NZ):
        waves = waves + zern_ref[slit, z] * basis_ref[z]
    inside = basis_ref[NZ]
    angle = 2.0 * math.pi * waves
    pr = inside * jnp.cos(angle)
    pi = inside * jnp.sin(angle)
    p40 = (pr[80:81, 40:41], pi[80:81, 40:41])
    m40 = (pr[0:1, 40:41], pi[0:1, 40:41])
    q40 = (pr[40:41, 80:81], pi[40:41, 80:81])
    n40 = (pr[40:41, 0:1], pi[40:41, 0:1])
    pupil = jnp.concatenate([pr, pi], axis=1)
    pupil = jnp.concatenate([pupil, jnp.zeros((KB - DISC, 2 * KB), F32)], axis=0)
    hat = forward_turn(left_mul(left_full[...], right_mul(pupil, full[...], 3), 3))
    pre_ref[...] = hat[0]
    pim_ref[...] = hat[1]
    total = jnp.sum(weight_ref[...], axis=1, keepdims=True)
    weight = weight_ref[...] / (math.pi * RAD * RAD * total)
    px = SHIFT - points_ref[0:1, :]
    py = SHIFT - points_ref[1:2, :]
    count = points_ref.shape[1]
    hot_x = lax.broadcasted_iota(jnp.int32, (LP, count), 0) == px
    hot_y = (lax.broadcasted_iota(jnp.int32, (KB, count), 0) % LP) == py
    omega = nt_mul(jnp.where(hot_x, weight, 0.0), jnp.where(hot_y, 1.0, 0.0))
    omega_cat = jnp.concatenate([omega[i : i + 1] for i in range(LAGS)], axis=1)

    def times(scalar, re, im, conj):
        a, b = scalar
        b = -b if conj else b
        return a * re - b * im, a * im + b * re

    def start(k, carry):
        re, im = block_ref[0, k], block_ref[1, k]
        x = jnp.concatenate([re, im], axis=1)
        hr, hi = forward_turn(left_mul(left_full[...], right_mul(x, full[...], 1), 1))
        cr, ci = pre_ref[...], pim_ref[...]
        prod = jnp.concatenate([cr * hr + ci * hi, cr * hi - ci * hr], axis=1)
        c = right_mul(inverse_turn(left_mul(left_inv[...], prod, 1)), inv_lag[...], 1)
        low = lane2 < LAGS
        er = jnp.where(low, pltpu.roll(re[0:1], KB - 40, 1), 0.0)
        ei = jnp.where(low, pltpu.roll(im[0:1], KB - 40, 1), 0.0)
        er, ei = times(p40, er, ei, True)
        edge = er + pltpu.roll(ei, LP, 1)
        rows = lax.broadcasted_iota(jnp.int32, (LP, KB), 0)
        lanes = lax.broadcasted_iota(jnp.int32, (LP, KB), 1)
        c = c - jnp.where(rows == LAGS - 1, edge, 0.0)
        fr, fi = times(q40, re[40 : 40 + LP, 0:1], im[40 : 40 + LP, 0:1], True)
        fall = jnp.where(lanes == LAGS - 1, fr, 0.0) + jnp.where(lanes == LP + LAGS - 1, fi, 0.0)
        z_ref[pl.ds(pl.multiple_of(k * LP, LP), LP), :] = c - jnp.where(rows < LAGS, fall, 0.0)
        return carry

    lax.fori_loop(0, NR, start, 0)

    def load_cat(ref):
        return jnp.concatenate(
            [ref[pl.ds(i, NR, stride=LP), :] for i in range(LAGS)], axis=1
        )

    def store_cat(ref, value):
        for i in range(LAGS):
            ref[pl.ds(i, NR, stride=LP), :] = value[:, i * KB : (i + 1) * KB]

    y_ref[...] = jnp.zeros_like(y_ref)
    power_re, power_im = pre_ref[...], pim_ref[...]
    u_ref[...] = power_re * power_re + power_im * power_im
    ycat = load_cat(z_ref) * omega_cat
    store_cat(y_ref, ycat)

    def apply_gram():
        s_ref[...] = right_mul(y_ref[...], lag[...], gpasses)

        def body(k, carry):
            at = pl.ds(pl.multiple_of(k * LP, LP), LP)
            hr, hi = forward_turn(left_mul(left_lag[...], s_ref[at, :], gpasses))
            power = u_ref[...]
            prod = jnp.concatenate([power * hr, power * hi], axis=1)
            s_ref[at, :] = inverse_turn(left_mul(left_inv[...], prod, gpasses))
            return carry

        lax.fori_loop(0, NR, body, 0, unroll=2)
        z = right_mul(s_ref[...], inv_lag[...], gpasses).reshape(NR, LP, KB)
        y = y_ref[...].reshape(NR, LP, KB)
        lanes = lax.broadcasted_iota(jnp.int32, (1, KB), 1)
        rows = lax.broadcasted_iota(jnp.int32, (1, LP, KB), 1)
        lanes3 = lax.broadcasted_iota(jnp.int32, (1, LP, KB), 2)

        def turned(scalar_a, scalar_b, value):
            cr, ci = times(scalar_a, scalar_b[0], scalar_b[1], True)
            flat = value.reshape(value.shape[0] * value.shape[1], KB)
            swap = pltpu.roll(flat, LP, 1).reshape(value.shape)
            sign = jnp.where(lanes < LP, -1.0, 1.0)
            return cr * value + (ci * sign) * swap

        first, last = y[:, 0:1], y[:, LAGS - 1 : LAGS]
        z = z - jnp.where(rows == 0, turned(m40, p40, last), 0.0)
        z = z - jnp.where(rows == LAGS - 1, last + turned(p40, m40, first), 0.0)
        ar, ai = times(n40, q40[0], q40[1], True)
        lr, li = y[:, :, LAGS - 1 : LAGS], y[:, :, LP + LAGS - 1 : LP + LAGS]
        gr, gi = y[:, :, 0:1], y[:, :, LP : LP + 1]
        z = z - jnp.where(lanes3 == 0, ar * lr - ai * li, 0.0)
        z = z - jnp.where(lanes3 == LP, ar * li + ai * lr, 0.0)
        z = z - jnp.where(lanes3 == LAGS - 1, lr + ar * gr + ai * gi, 0.0)
        z = z - jnp.where(lanes3 == LP + LAGS - 1, li + ar * gi - ai * gr, 0.0)
        z_ref[...] = z.reshape(NR * LP, KB)

    eye = lax.broadcasted_iota(jnp.int32, (NR, NR), 0) == lax.broadcasted_iota(
        jnp.int32, (NR, NR), 1
    )

    def trace_of(m):
        return jnp.sum(
            jnp.sum(jnp.where(eye, m, 0.0), axis=1, keepdims=True), axis=0, keepdims=True
        )

    for it in range(ITERS):
        apply_gram()
        yc, zc = load_cat(y_ref), load_cat(z_ref)
        gram = nt_mul(yc, zc)
        ridge = RIDGE_SHARE * trace_of(gram) / NR + 1e-06
        gram = gram + jnp.where(eye, ridge, 0.0)
        inverse = eliminate(gram, 0.0)[:, NR : 2 * NR]
        projected = small_mul(inverse, zc)
        if it < ITERS - 1:
            store_cat(y_ref, projected * omega_cat)
        else:
            mixing = nt_mul(projected * omega_cat, projected)
            upper = eliminate(mixing, 1e-6 * trace_of(mixing))[:, :NR]
            store_cat(y_ref, small_mul(small_mul(upper, inverse), yc))

    def finish(k, carry):
        y = y_ref[pl.ds(pl.multiple_of(k * LP, LP), LP), :]
        hr, hi = forward_turn(left_mul(left_lag[...], right_mul(y, lag[...], 1), 1))
        cr, ci = pre_ref[...], pim_ref[...]
        prod = jnp.concatenate([cr * hr - ci * hi, cr * hi + ci * hr], axis=1)
        a = right_mul(inverse_turn(left_mul(left_full[...], prod, 1)), inv_full[...], 1)
        last = y[LAGS - 1 : LAGS]
        er = pltpu.roll(jnp.where(lane2 < LP, last, 0.0), 40, 1)
        ei = pltpu.roll(jnp.where(lane2 < LP, 0.0, last), 40 + LP, 1)
        er, ei = times(p40, er, ei, False)
        fr, fi = times(
            q40, y[:, LAGS - 1 : LAGS], y[:, LP + LAGS - 1 : LP + LAGS], False
        )
        rows = lax.broadcasted_iota(jnp.int32, (KB, KB), 0)
        lanes = lax.broadcasted_iota(jnp.int32, (KB, KB), 1)

        def place(column):
            wide = jnp.where(lax.broadcasted_iota(jnp.int32, (LP, KB), 1) == 0, column, 0.0)
            return jnp.concatenate(
                [jnp.zeros((40, KB), F32), wide, jnp.zeros((KB - 40 - LP, KB), F32)], axis=0
            )

        re = a[:, :KB] - jnp.where(rows == 0, er, 0.0) - place(fr)
        im = a[:, KB:] - jnp.where(rows == 0, ei, 0.0) - place(fi)
        out_ref[k] = jnp.concatenate([re, im], axis=1).astype(BF16)
        return carry

    lax.fori_loop(0, NR, finish, 0)


def synthesize(slit, zernike, start_block, source_points, source_weight, gpasses=1):
    tables = [jnp.asarray(t) for t in dft_tables()]
    smem = pl.BlockSpec(memory_space=pltpu.SMEM)
    vmem = pl.BlockSpec(memory_space=pltpu.VMEM)
    return pl.pallas_call(
        functools.partial(synth_kernel, gpasses=gpasses),
        out_shape=jax.ShapeDtypeStruct((NR, KB, 2 * KB), BF16),
        in_specs=[smem, smem] + [vmem] * 11,
        out_specs=vmem,
        scratch_shapes=[
            pltpu.VMEM((NR * LP, KB), F32),
            pltpu.VMEM((NR * LP, KB), F32),
            pltpu.VMEM((NR * LP, 2 * KB), F32),
            pltpu.VMEM((KB, KB), F32),
            pltpu.VMEM((KB, KB), F32),
            pltpu.VMEM((KB, KB), F32),
        ],
        compiler_params=pltpu.CompilerParams(vmem_limit_bytes=50 * 2**20),
        cost_estimate=pl.CostEstimate(
            flops=6 * 10**9, bytes_accessed=8 * 10**6, transcendentals=0
        ),
    )(
        slit, zernike, jnp.asarray(zernike_table()), start_block,
        source_points.T, source_weight[None, :], *tables,
    )


@functools.lru_cache(None)
def phase_tables():
    frequency = np.arange(KB) - KB // 2

    def make(period):
        angle = 2.0 * np.pi / period * np.mod(np.arange(period)[:, None] * frequency, period)
        return [
            turn(angle.astype(np.float32)).astype(ml_dtypes.bfloat16) for turn in (np.cos, np.sin)
        ]

    return make(TS) + make(TS + 2 * HALO)


def row_phases(rank, rows):
    cosine, sine = phase_tables()[:2]
    turn = np.concatenate([cosine, sine], axis=1)
    return lax.dynamic_slice_in_dim(jnp.asarray(turn), rank * rows, rows, 0)


def image_kernel(
    *refs, tiles, rows, scale,
):
    kernel_refs = refs[:tiles]
    (spec_ref, target_ref, turn_ref, back_ref, inverse_ref, adjoint_ref,
     resist_ref, grad_ref, wave_ref, field_ref) = refs[tiles:]

    def parts(block):
        return block[:, :KB].astype(F32), block[:, KB:].astype(F32)

    for t in range(tiles):
        kernels = kernel_refs[t]
        sre = scale * spec_ref[0, t].astype(F32)
        sim = scale * spec_ref[1, t].astype(F32)

        def forward(pair, carry):
            w = []
            for q in range(2):
                kr, ki = parts(kernels[2 * pair + q])
                w.append(((kr * sre + ki * sim).astype(BF16), (kr * sim - ki * sre).astype(BF16)))
            both = jnp.concatenate(
                [jnp.concatenate([w[0][h], w[1][h]], axis=1) for h in range(2)], axis=0
            )
            turned = jnp.dot(turn_ref[...], both, preferred_element_type=F32).astype(BF16)
            for q in range(2):
                at = pl.ds(pl.multiple_of((2 * pair + q) * rows, rows), rows)
                lanes = slice(q * KB, (q + 1) * KB)
                wave_ref[at, :] = jnp.concatenate(
                    [turned[:rows, lanes], turned[rows:, lanes]], axis=1
                )
            return carry

        lax.fori_loop(0, NR // 2, forward, 0, unroll=2)
        field_ref[...] = jnp.dot(wave_ref[...], inverse_ref[...], preferred_element_type=F32)
        intensity = jnp.zeros((rows, TS), F32)
        for k in range(NR):
            field = field_ref[k * rows : (k + 1) * rows, :]
            intensity = intensity + field * field
        resist = 1.0 / (1.0 + jnp.exp(-STEEPNESS * (intensity - THRESHOLD)))
        goal = target_ref[:, t * TS : (t + 1) * TS].astype(F32)
        resist_ref[:, t * TS : (t + 1) * TS] = resist.astype(BF16)
        slope = 4.0 * (resist - goal) * STEEPNESS * resist * (1.0 - resist)
        for k in range(NR):
            at = slice(k * rows, (k + 1) * rows)
            wave_ref[at, :] = (field_ref[at, :] * slope).astype(BF16)
        wave_ref[...] = jnp.dot(
            wave_ref[...], adjoint_ref[...], preferred_element_type=F32
        ).astype(BF16)

        def adjoint(pair, carry):
            acc_re, acc_im = carry
            waves = [
                wave_ref[pl.ds(pl.multiple_of((2 * pair + q) * rows, rows), rows), :]
                for q in range(2)
            ]
            both = jnp.concatenate(
                [
                    jnp.concatenate([waves[q][:, h * KB : (h + 1) * KB] for q in range(2)], axis=1)
                    for h in range(2)
                ],
                axis=0,
            )
            turned = jnp.dot(back_ref[...], both, preferred_element_type=F32)
            for q in range(2):
                kr, ki = parts(kernels[2 * pair + q])
                tr = turned[:KB, q * KB : (q + 1) * KB]
                ti = turned[KB:, q * KB : (q + 1) * KB]
                acc_re = acc_re + kr * tr + ki * ti
                acc_im = acc_im + ki * tr - kr * ti
            return acc_re, acc_im

        zero = jnp.zeros((KB, KB), F32)
        acc_re, acc_im = lax.fori_loop(0, NR // 2, adjoint, (zero, zero))
        grad_ref[t, 0] = acc_re.astype(BF16)
        grad_ref[t, 1] = acc_im.astype(BF16)


def image(kernels, spectra, target, phases, scale):
    tiles = len(kernels)
    rows = target.shape[0]
    c, s = phases[:, :KB], phases[:, KB:]
    turn = jnp.concatenate(
        [jnp.concatenate([c, -s], axis=1), jnp.concatenate([s, c], axis=1)], axis=0
    )
    back = jnp.concatenate(
        [jnp.concatenate([c.T, -s.T], axis=1), jnp.concatenate([s.T, c.T], axis=1)], axis=0
    )
    cosine, sine = [table[HALO : HALO + TS] for table in phase_tables()[2:]]
    inverse = jnp.asarray(np.concatenate([cosine, -sine], axis=1).T.copy())
    adjoint = jnp.asarray(np.concatenate([cosine, sine], axis=1))
    vmem = pl.BlockSpec(memory_space=pltpu.VMEM)
    return pl.pallas_call(
        functools.partial(image_kernel, tiles=tiles, rows=rows, scale=scale),
        out_shape=(
            jax.ShapeDtypeStruct(target.shape, BF16),
            jax.ShapeDtypeStruct((tiles, 2, KB, KB), BF16),
        ),
        in_specs=[vmem] * (tiles + 6),
        out_specs=(vmem, vmem),
        scratch_shapes=[
            pltpu.VMEM((NR * rows, TS), BF16),
            pltpu.VMEM((NR * rows, TS), F32),
        ],
        compiler_params=pltpu.CompilerParams(vmem_limit_bytes=50 * 2**20),
        cost_estimate=pl.CostEstimate(
            flops=2 * 10**9, bytes_accessed=4 * 10**6, transcendentals=0
        ),
    )(*kernels, spectra, target, turn, back, inverse, adjoint)


def patch_gradient(grad_re, grad_im, spectrum_scale, row_table, column_forward):
    back_re = (spectrum_scale * grad_re).astype(jnp.bfloat16)
    back_im = (spectrum_scale * grad_im).astype(jnp.bfloat16)
    back_block = jnp.concatenate(
        [jnp.concatenate([back_re, back_im], axis=1), jnp.concatenate([-back_im, back_re], axis=1)],
        axis=0,
    )
    back_rows = jnp.dot(row_table, back_block, preferred_element_type=jnp.float32).astype(
        jnp.bfloat16
    )
    return jnp.dot(back_rows, column_forward.T, preferred_element_type=jnp.float32)


def tile_kernels(tile_slit, zernike, start_block, source_points, source_weight):
    tiles_here = tile_slit.shape[0]
    group_size = lax.axis_size("src")
    rank = lax.axis_index("src")
    make = lambda slit: synthesize(slit, zernike, start_block, source_points, source_weight)
    if group_size % tiles_here:
        return [make(tile_slit[t : t + 1]) for t in range(tiles_here)]
    place = rank % tiles_here
    own = make(lax.dynamic_slice_in_dim(tile_slit, place, 1, 0))
    held = [own]
    for shift in range(1, tiles_here):
        pairs = [
            (i, i - i % tiles_here + (i + shift) % tiles_here) for i in range(group_size)
        ]
        held.append(lax.ppermute(own, "src", pairs))
    result = []
    for t in range(tiles_here):
        take = held[0]
        for shift in range(1, tiles_here):
            take = jnp.where((place - shift) % tiles_here == t, held[shift], take)
        result.append(take)
    return result


def on_device(mask, target, start_block, zernike, source_points, source_weight, tile_slit):
    group_rank = lax.axis_index("src")
    rows_here = mask.shape[0]
    width_here = mask.shape[1]
    tiles_here = tile_slit.shape[0]
    kernels = tile_kernels(tile_slit, zernike, start_block, source_points, source_weight)
    extended = with_halo(mask, (("tile", 1),), HALO)
    patch_width = TS + 2 * HALO
    spectrum_scale = 1.0 / math.sqrt(TS * patch_width)
    row_table = row_phases(group_rank, rows_here)
    cosine, sine = phase_tables()[2:]
    column_forward = jnp.asarray(np.concatenate([cosine, -sine], axis=1))
    patches = jnp.stack(
        [extended[:, counter * TS : counter * TS + patch_width] for counter in range(tiles_here)]
    )
    columns = jnp.einsum(
        "jxy,yc->jxc", patches, column_forward, preferred_element_type=jnp.float32
    ).astype(jnp.bfloat16)
    row_sums = jnp.einsum("xc,jxd->jcd", row_table, columns, preferred_element_type=jnp.float32)
    partial_re = row_sums[:, :KB, :KB] + row_sums[:, KB:, KB:]
    partial_im = row_sums[:, :KB, KB:] - row_sums[:, KB:, :KB]
    partial = jnp.stack([partial_re, partial_im]).astype(jnp.bfloat16)
    summed = lax.psum(partial, "src")
    resist, grads = image(kernels, summed, target, row_table, spectrum_scale)
    total = lax.psum(grads, "src").astype(jnp.float32)
    accumulated = jnp.zeros((rows_here, width_here + 2 * HALO), jnp.float32)
    for counter in range(tiles_here):
        patch_grad = patch_gradient(
            total[counter, 0], total[counter, 1], spectrum_scale, row_table, column_forward
        )
        accumulated = accumulated.at[:, counter * TS : counter * TS + patch_width].add(patch_grad)
    rim_cols = jnp.concatenate([accumulated[:, :HALO], accumulated[:, width_here + HALO :]], axis=1)
    beside_all = with_halo(rim_cols.astype(jnp.bfloat16), (("tile", 1),), HALO).astype(
        rim_cols.dtype
    )
    from_left = beside_all[:, :HALO]
    from_right = beside_all[:, 3 * HALO :]
    inner_part = accumulated[:, HALO : HALO + width_here]
    inner_part = (
        inner_part
        + jnp.pad(from_left, ((0, 0), (0, width_here - HALO)))
        + jnp.pad(from_right, ((0, 0), (width_here - HALO, 0)))
    )
    return (resist, inner_part.astype(jnp.bfloat16))


def solution(mesh):
    placed = (P("src", "tile"), P("src", "tile"), P(), P(), P(), P(), P("tile"))
    return jax.shard_map(
        on_device,
        mesh=mesh,
        in_specs=placed,
        out_specs=(P("src", "tile"), P("src", "tile")),
        check_vma=False,
    )
```

```python
import functools
import math

import jax
import jax.numpy as jnp
import ml_dtypes
import numpy as np
from jax import lax
from jax.experimental import pallas as pl
from jax.experimental.pallas import tpu as pltpu
from jax.sharding import PartitionSpec as P

KB = 128
NR = 24
NZ = 37
RAD = 40
SHIFT = 24
HALO = 64
ITERS = 4
TS = 256
LAGS = 2 * SHIFT + 1
LP = 64
DISC = 88

STEEPNESS = 4.0
THRESHOLD = 0.5
RIDGE_SHARE = 0.001
F32 = jnp.float32
BF16 = jnp.bfloat16


def with_halo(cells, sides, width):
    for axis, dim in sides:
        count = lax.axis_size(axis)
        ends = count - 1
        head = lax.slice_in_dim(cells, 0, width, axis=dim)
        tail = lax.slice_in_dim(cells, cells.shape[dim] - width, cells.shape[dim], axis=dim)
        cells = jnp.concatenate(
            [
                lax.ppermute(tail, axis, [(i, (i + 1) % count) for i in range(ends)]),
                cells,
                lax.ppermute(head, axis, [((i + 1) % count, i) for i in range(ends)]),
            ],
            axis=dim,
        )
    return cells


def noll_terms(term_count):
    listing = []
    degree = 0
    while len(listing) < term_count:
        for azimuth in range(degree % 2, degree + 1, 2):
            if azimuth == 0:
                listing.append((degree, 0, 0))
            else:
                for repeat in range(2):
                    number = len(listing) + 1
                    listing.append((degree, azimuth, 2 if number % 2 == 0 else 1))
        degree += 1
    return listing[:term_count]


def radial_terms(degree, azimuth):
    powers = []
    for counter in range((degree - azimuth) // 2 + 1):
        factor = (
            (-1) ** counter
            * math.factorial(degree - counter)
            / (
                math.factorial(counter)
                * math.factorial((degree + azimuth) // 2 - counter)
                * math.factorial((degree - azimuth) // 2 - counter)
            )
        )
        powers.append((degree - 2 * counter, factor))
    return powers


@functools.lru_cache(None)
def zernike_table():
    u = (np.arange(DISC) - RAD)[:, None]
    v = (np.arange(KB) - RAD)[None, :]
    inside = (u * u + v * v <= RAD * RAD).astype(np.float64)
    rho = np.sqrt(u * u + v * v) / RAD
    theta = np.arctan2(v + 0.0 * u, u + 0.0 * v)
    planes = []
    for degree, azimuth, parity in noll_terms(NZ):
        radial = sum(f * rho**e for e, f in radial_terms(degree, azimuth))
        if azimuth == 0:
            plane = math.sqrt(degree + 1.0) * radial
        else:
            turn = np.cos if parity == 2 else np.sin
            plane = math.sqrt(2.0 * degree + 2.0) * radial * turn(azimuth * theta)
        planes.append(plane * inside)
    planes.append(inside)
    return np.stack(planes).astype(np.float32)


@functools.lru_cache(None)
def dft_tables():
    f = np.arange(KB)
    angle = 2.0 * np.pi / KB * ((f[:, None] * f[None, :]) % KB)
    return np.cos(angle).astype(np.float32), np.sin(angle).astype(np.float32)


def halves(x):
    high = x.astype(BF16)
    return high, (x - high.astype(F32)).astype(BF16)


def dot(x, y):
    return jnp.dot(x.astype(BF16), y.astype(BF16), preferred_element_type=F32)


def nt_mul(x, y):
    xh, xl = halves(x)
    yh, yl = halves(y)
    dims = (((1,), (1,)), ((), ()))
    return (
        lax.dot_general(xh, yh, dims, preferred_element_type=F32)
        + lax.dot_general(xl, yh, dims, preferred_element_type=F32)
        + lax.dot_general(xh, yl, dims, preferred_element_type=F32)
    )


def small_mul(m, x):
    mh, ml = halves(m)
    xh, xl = halves(x)
    return (
        jnp.dot(mh, xh, preferred_element_type=F32)
        + jnp.dot(ml, xh, preferred_element_type=F32)
        + jnp.dot(mh, xl, preferred_element_type=F32)
    )


def forward_turn(t):
    n = t.shape[0] // 2
    return t[:n, :KB] + t[n:, KB:], t[:n, KB:] - t[n:, :KB]


def inverse_turn(t):
    n = t.shape[0] // 2
    return jnp.concatenate([t[:n, :KB] - t[n:, KB:], t[:n, KB:] + t[n:, :KB]], axis=1)


def exact_dot(x, y):
    xh, xl = halves(x)
    yh, yl = halves(y)
    return dot(xh, yh) + dot(xl, yh) + dot(xh, yl)


def lane_join(parts):
    return jnp.concatenate(parts, axis=1)


def row_join(parts):
    return jnp.concatenate(parts, axis=0)


def eliminate(gram, floor):
    row = lax.broadcasted_iota(jnp.int32, (NR, KB), 0)
    lane = lax.broadcasted_iota(jnp.int32, (NR, KB), 1)
    aug = lane_join([gram, jnp.zeros((NR, KB - NR), F32)])
    aug = aug + jnp.where(lane == row + NR, 1.0, 0.0)
    scales = jnp.zeros((NR, KB), F32)
    block = 4
    for begin in range(0, NR, block):
        cols = [
            jnp.broadcast_to(aug[:, j : j + 1], (NR, KB)) for j in range(begin, begin + block)
        ]
        for m in range(block):
            j = begin + m
            pivot = cols[m][j : j + 1, :]
            good = pivot > floor
            safe = jnp.where(good, pivot, 1.0)
            inverse = jnp.where(good, 1.0 / safe, 0.0)
            root = jnp.where(good, lax.rsqrt(safe), 0.0)
            factor = jnp.where(row > j, cols[m] * inverse, 0.0)
            aug = aug - factor * aug[j : j + 1, :]
            for later in range(m + 1, block):
                cols[later] = cols[later] - factor * cols[later][j : j + 1, :]
            scales = jnp.where(row == j, root, scales)
    return aug * scales


GROUP = 8


def synth_kernel(
    coef_ref, points_ref, weight_ref, basis_hbm, cos_hbm, sin_hbm, block_hbm,
    out_ref,
    basis_ref, cos_ref, sin_ref, block_ref,
    full, left_full, lag, inv_lag, inv_full, left_lag, left_inv,
    y_ref, z_ref, power_ref, pre_ref, pim_ref, edge_ref, sems,
):
    sources = (basis_hbm, cos_hbm, sin_hbm, block_hbm)
    targets = (basis_ref, cos_ref, sin_ref, block_ref)
    copies = [
        pltpu.make_async_copy(a, b, sems.at[i]) for i, (a, b) in enumerate(zip(sources, targets))
    ]
    for copy in copies:
        copy.start()
    lane = lax.broadcasted_iota(jnp.int32, (1, KB), 1)
    total = jnp.sum(weight_ref[...], axis=1, keepdims=True)
    weight = weight_ref[...] / (math.pi * RAD * RAD * total)
    px = SHIFT - points_ref[0:1, :]
    py = SHIFT - points_ref[1:2, :]
    count = points_ref.shape[1]
    hot_x = lax.broadcasted_iota(jnp.int32, (LP, count), 0) == px
    lag_lane = lax.broadcasted_iota(jnp.int32, (KB, count), 0)
    hot_y = jnp.where(lag_lane < LP, lag_lane, lag_lane - LP) == py
    omega = nt_mul(jnp.where(hot_x, weight, 0.0), jnp.where(hot_y, 1.0, 0.0))
    omega_cat = lane_join([omega[i : i + 1] for i in range(LAGS)])
    copies[0].wait()
    waves = coef_ref[0, 0] * basis_ref[0]
    for z in range(1, NZ):
        waves = waves + coef_ref[0, z] * basis_ref[z]
    inside = basis_ref[NZ]
    angle = 2.0 * math.pi * waves
    pr = inside * jnp.cos(angle)
    pi = inside * jnp.sin(angle)
    p40 = (pr[80:81, 40:41], pi[80:81, 40:41])
    m40 = (pr[0:1, 40:41], pi[0:1, 40:41])
    q40 = (pr[40:41, 80:81], pi[40:41, 80:81])
    n40 = (pr[40:41, 0:1], pi[40:41, 0:1])
    for copy in copies[1:3]:
        copy.wait()
    c, s = cos_ref[...], sin_ref[...]
    scale = 1.0 / (KB * KB)
    full32 = row_join([lane_join([c, -s]), lane_join([s, c])])
    left32 = row_join([c, s])
    full[...] = full32.astype(BF16)
    left_full[...] = left32.astype(BF16)
    inv_full[...] = (scale * row_join([lane_join([c, s]), lane_join([-s, c])])).astype(BF16)
    keep_row = lax.broadcasted_iota(jnp.int32, (LP, KB), 0) < LAGS
    cy, sy = jnp.where(keep_row, c[:LP], 0.0), jnp.where(keep_row, s[:LP], 0.0)
    lag[...] = row_join([lane_join([cy, -sy]), lane_join([sy, cy])]).astype(BF16)
    left_inv[...] = row_join([cy, sy]).astype(BF16)
    keep_lane = lax.broadcasted_iota(jnp.int32, (KB, KB), 1) < LAGS
    ct, st = jnp.where(keep_lane, scale * c, 0.0), jnp.where(keep_lane, scale * s, 0.0)
    inv_lag[...] = row_join(
        [ct + pltpu.roll(st, LP, 1), pltpu.roll(ct, LP, 1) - st]
    ).astype(BF16)
    left_lag[...] = row_join([c[:, :LP], s[:, :LP]]).astype(BF16)
    pupil = row_join([lane_join([pr, pi]), jnp.zeros((KB - DISC, 2 * KB), F32)])
    hat = forward_turn(exact_dot(left32, exact_dot(pupil, full32)))
    pre_ref[...] = hat[0]
    pim_ref[...] = hat[1]
    power_ref[...] = hat[0] * hat[0] + hat[1] * hat[1]

    def times(scalar, re, im, conj):
        a, b = scalar
        b = -b if conj else b
        return a * re - b * im, a * im + b * re

    def entries(shape, items):
        row = lax.broadcasted_iota(jnp.int32, shape, 0)
        col = lax.broadcasted_iota(jnp.int32, shape, 1)
        matrix = jnp.zeros(shape, F32)
        for i, j, value in items:
            matrix = matrix + jnp.where((row == i) & (col == j), value, 0.0)
        return matrix.astype(BF16)

    end = LAGS - 1
    qr, qi = q40
    ar, ai = times(n40, qr, qi, True)
    start_fix = entries(
        (2 * KB, KB),
        [(0, end, -qr), (KB, end, -qi), (0, LP + end, qi), (KB, LP + end, -qr)],
    )
    gram_fix = entries(
        (KB, KB),
        [
            (end, 0, -ar), (LP + end, 0, ai), (LP + end, LP, -ar), (end, LP, -ai),
            (end, end, -1.0), (0, end, -ar), (LP, end, -ai),
            (LP + end, LP + end, -1.0), (LP, LP + end, -ar), (0, LP + end, ai),
        ],
    )
    final_fix = entries(
        (KB, 2 * KB),
        [(end, 0, -qr), (LP + end, 0, qi), (end, KB, -qi), (LP + end, KB, -qr)],
    )

    copies[3].wait()
    left = left_full[...]
    right = full[...]

    def lanes_of(x, g, width):
        return x[:, g * width : (g + 1) * width]

    def start(group, carry):
        base = group * GROUP
        xs = [
            lane_join([block_ref[0, base + g].astype(BF16), block_ref[1, base + g].astype(BF16)])
            for g in range(GROUP)
        ]
        one = dot(row_join(xs), right).astype(BF16)
        two = dot(left, lane_join([one[g * KB : (g + 1) * KB] for g in range(GROUP)]))
        cr, ci = pre_ref[...], pim_ref[...]
        prods = []
        for g in range(GROUP):
            hr, hi = forward_turn(lanes_of(two, g, 2 * KB))
            prods += [(cr * hr + ci * hi).astype(BF16), (cr * hi - ci * hr).astype(BF16)]
        three = dot(left_inv[...], lane_join(prods))
        four = row_join(
            [
                lane_join([inverse_turn(lanes_of(three, g, 2 * KB)).astype(BF16), xs_rows])
                for g, xs_rows in enumerate([x.astype(F32)[40 : 40 + LP].astype(BF16) for x in xs])
            ]
        )
        c = dot(four, row_join([inv_lag[...], start_fix]))
        z_ref[pl.ds(pl.multiple_of(base * LP, GROUP * LP), GROUP * LP), :] = c
        return carry

    lax.fori_loop(0, NR // GROUP, start, 0)
    at_first = pl.ds(0, NR, stride=LP)
    at_last = pl.ds(end, NR, stride=LP)
    within = lane < LAGS
    er = row_join([block_ref[0, k, 0:1, :] for k in range(NR)])
    ei = row_join([block_ref[1, k, 0:1, :] for k in range(NR)])
    er = jnp.where(within, pltpu.roll(er, KB - 40, 1), 0.0)
    ei = jnp.where(within, pltpu.roll(ei, KB - 40, 1), 0.0)
    er, ei = times(p40, er, ei, True)
    z_ref[at_last, :] = z_ref[at_last, :] - (er + pltpu.roll(ei, LP, 1))

    def load_cat(ref):
        return lane_join([ref[pl.ds(i, NR, stride=LP), :] for i in range(LAGS)])

    def store_cat(ref, value):
        for i in range(LAGS):
            ref[pl.ds(i, NR, stride=LP), :] = value[:, i * KB : (i + 1) * KB]

    y_ref[...] = jnp.zeros_like(y_ref)
    store_cat(y_ref, load_cat(z_ref) * omega_cat)

    def turned(scalar_a, scalar_b, value):
        cr, ci = times(scalar_a, scalar_b[0], scalar_b[1], True)
        return cr * value + jnp.where(lane < LP, -ci, ci) * pltpu.roll(value, LP, 1)

    def apply_gram():
        def body(group, carry):
            base = pl.multiple_of(group * GROUP * LP, GROUP * LP)
            at = pl.ds(base, GROUP * LP)
            y = y_ref[at, :].astype(BF16)
            one = dot(y, lag[...]).astype(BF16)
            two = dot(
                left_lag[...], lane_join([one[g * LP : (g + 1) * LP] for g in range(GROUP)])
            )
            power = power_ref[...]
            prods = []
            for g in range(GROUP):
                hr, hi = forward_turn(lanes_of(two, g, 2 * KB))
                prods += [(power * hr).astype(BF16), (power * hi).astype(BF16)]
            three = dot(left_inv[...], lane_join(prods))
            four = row_join(
                [inverse_turn(lanes_of(three, g, 2 * KB)).astype(BF16) for g in range(GROUP)]
            )
            z_ref[at, :] = dot(lane_join([four, y]), row_join([inv_lag[...], gram_fix]))
            return carry

        lax.fori_loop(0, NR // GROUP, body, 0)
        y_first, y_last = y_ref[at_first, :], y_ref[at_last, :]
        z_ref[at_first, :] = z_ref[at_first, :] - turned(m40, p40, y_last)
        z_ref[at_last, :] = z_ref[at_last, :] - (y_last + turned(p40, m40, y_first))

    eye = lax.broadcasted_iota(jnp.int32, (NR, NR), 0) == lax.broadcasted_iota(
        jnp.int32, (NR, NR), 1
    )

    def trace_of(m):
        return jnp.sum(
            jnp.sum(jnp.where(eye, m, 0.0), axis=1, keepdims=True), axis=0, keepdims=True
        )

    for it in range(ITERS):
        apply_gram()
        yc, zc = load_cat(y_ref), load_cat(z_ref)
        gram = nt_mul(yc, zc)
        ridge = RIDGE_SHARE * trace_of(gram) / NR + 1e-06
        gram = gram + jnp.where(eye, ridge, 0.0)
        inverse = eliminate(gram, 0.0)[:, NR : 2 * NR]
        projected = small_mul(inverse, zc)
        if it < ITERS - 1:
            store_cat(y_ref, projected * omega_cat)
        else:
            mixing = nt_mul(projected * omega_cat, projected)
            upper = eliminate(mixing, 1e-6 * trace_of(mixing))[:, :NR]
            store_cat(y_ref, small_mul(small_mul(upper, inverse), yc))

    last = y_ref[at_last, :]
    er = pltpu.roll(jnp.where(lane < LP, last, 0.0), 40, 1)
    ei = pltpu.roll(jnp.where(lane < LP, 0.0, last), 40 + LP, 1)
    er, ei = times(p40, er, ei, False)
    edge_ref[...] = lane_join([er, ei])

    def finish(group, carry):
        base = group * GROUP
        y = y_ref[pl.ds(pl.multiple_of(base * LP, GROUP * LP), GROUP * LP), :].astype(BF16)
        one = dot(y, lag[...]).astype(BF16)
        two = dot(left_lag[...], lane_join([one[g * LP : (g + 1) * LP] for g in range(GROUP)]))
        cr, ci = pre_ref[...], pim_ref[...]
        prods = []
        for g in range(GROUP):
            hr, hi = forward_turn(lanes_of(two, g, 2 * KB))
            prods += [(cr * hr - ci * hi).astype(BF16), (cr * hi + ci * hr).astype(BF16)]
        three = dot(left, lane_join(prods))
        four = row_join(
            [inverse_turn(lanes_of(three, g, 2 * KB)).astype(BF16) for g in range(GROUP)]
        )
        a = dot(four, inv_full[...])
        fix = dot(y, final_fix)
        edges = edge_ref[pl.ds(pl.multiple_of(base, GROUP), GROUP), :]
        for g in range(GROUP):
            top = g * KB
            head = a[top : top + 8]
            first_row = lax.broadcasted_iota(jnp.int32, head.shape, 0) == 0
            head = head - jnp.where(first_row, edges[g : g + 1], 0.0)
            out_ref[base + g] = row_join(
                [
                    head,
                    a[top + 8 : top + 40],
                    a[top + 40 : top + 40 + LP] + fix[g * LP : (g + 1) * LP],
                    a[top + 40 + LP : top + KB],
                ]
            ).astype(BF16)
        return carry

    lax.fori_loop(0, NR // GROUP, finish, 0)


def synthesize(slit, zernike, start_block, source_points, source_weight):
    basis = jnp.asarray(zernike_table())
    cosine, sine = [jnp.asarray(t) for t in dft_tables()]
    smem = pl.BlockSpec(memory_space=pltpu.SMEM)
    vmem = pl.BlockSpec(memory_space=pltpu.VMEM)
    hbm = pl.BlockSpec(memory_space=pl.ANY)
    held = [basis, cosine, sine, start_block]
    tables = [(2 * KB, 2 * KB), (2 * KB, KB), (KB, 2 * KB), (2 * KB, KB),
              (2 * KB, 2 * KB), (2 * KB, LP), (KB, KB)]
    return pl.pallas_call(
        synth_kernel,
        out_shape=jax.ShapeDtypeStruct((NR, KB, 2 * KB), BF16),
        in_specs=[smem, vmem, vmem] + [hbm] * len(held),
        out_specs=vmem,
        scratch_shapes=[pltpu.VMEM(x.shape, x.dtype) for x in held]
        + [pltpu.VMEM(shape, BF16) for shape in tables]
        + [
            pltpu.VMEM((NR * LP, KB), F32),
            pltpu.VMEM((NR * LP, KB), F32),
            pltpu.VMEM((KB, KB), F32),
            pltpu.VMEM((KB, KB), F32),
            pltpu.VMEM((KB, KB), F32),
            pltpu.VMEM((NR, 2 * KB), F32),
            pltpu.SemaphoreType.DMA((len(held),)),
        ],
        compiler_params=pltpu.CompilerParams(vmem_limit_bytes=56 * 2**20),
        cost_estimate=pl.CostEstimate(
            flops=60 * 10**9, bytes_accessed=8 * 10**6, transcendentals=0
        ),
    )(
        lax.dynamic_slice_in_dim(zernike, slit[0], 1, 0),
        source_points.T, source_weight[None, :], *held,
    )


@functools.lru_cache(None)
def phase_tables():
    frequency = np.arange(KB) - KB // 2

    def make(period):
        angle = 2.0 * np.pi / period * np.mod(np.arange(period)[:, None] * frequency, period)
        return [
            turn(angle.astype(np.float32)).astype(ml_dtypes.bfloat16) for turn in (np.cos, np.sin)
        ]

    return make(TS) + make(TS + 2 * HALO)


@functools.lru_cache(None)
def imaging_tables(group):
    cosine, sine, column_cos, column_sin = [t.astype(np.float32) for t in phase_tables()]
    rows = TS // group
    turns, backs = [], []
    for rank in range(group):
        c, s = [t[rank * rows : (rank + 1) * rows] for t in (cosine, sine)]
        turns.append(np.block([[c, -s], [s, c]]))
        backs.append(np.block([[c.T, -s.T], [s.T, c.T]]))
    inner = slice(HALO, HALO + TS)
    inverse = np.concatenate([column_cos[inner], -column_sin[inner]], axis=1).T
    adjoint = np.concatenate([column_cos[inner], column_sin[inner]], axis=1)
    spread = np.concatenate([column_cos, -column_sin], axis=1).T
    return tuple(
        np.ascontiguousarray(t) for t in (np.stack(turns), np.stack(backs), inverse, adjoint, spread)
    )


def image_kernel(
    own_hbm, spec_ref, target_ref, turn_hbm, back_hbm, inverse_hbm, adjoint_hbm, spread_hbm,
    resist_ref, grad_ref,
    held, turn32, back32, inverse32, adjoint32, spread32,
    wave_ref, field_ref, part_ref, got_ref, acc_ref, rim_ref, left_ref, right_ref,
    local_sems, k_send, k_recv, g_send, g_recv, r_send, r_recv,
    *, group, line, tiles, rows, scale,
):
    rank, me = lax.axis_index("src"), lax.axis_index("tile")
    place = lax.rem(rank, tiles)
    right = lax.rem(me + 1, line)
    left = lax.rem(me + line - 1, line)
    loads = [
        (own_hbm, held.at[0]), (turn_hbm.at[rank], turn32), (back_hbm.at[rank], back32),
        (inverse_hbm, inverse32), (adjoint_hbm, adjoint32), (spread_hbm, spread32),
    ]
    loads = [pltpu.make_async_copy(a, b, local_sems.at[i]) for i, (a, b) in enumerate(loads)]
    for load in loads:
        load.start()

    peers = [lax.rem(rank + step, group) for step in range(1, group)]
    barrier = pltpu.get_barrier_semaphore()
    for peer in peers:
        pl.semaphore_signal(
            barrier, inc=1, device_id=(peer, me), device_id_type=pl.DeviceIdType.MESH
        )
    for side in (left, right):
        pl.semaphore_signal(
            barrier, inc=1, device_id=(rank, side), device_id_type=pl.DeviceIdType.MESH
        )
    pl.semaphore_wait(barrier, group - 1 + 2)

    def send(src, dst, send_sem, recv_sem, device):
        copy = pltpu.make_async_remote_copy(
            src_ref=src, dst_ref=dst, send_sem=send_sem, recv_sem=recv_sem,
            device_id=device, device_id_type=pl.DeviceIdType.MESH,
        )
        copy.start()
        return copy

    kernel_copies = [
        send(
            own_hbm, held.at[step], k_send.at[step - 1], k_recv.at[step - 1],
            (rank - place + lax.rem(place + step, tiles), me),
        )
        for step in range(1, tiles)
    ]
    for load in loads:
        load.wait()
    turn = turn32[...].astype(BF16)
    back = back32[...].astype(BF16)
    inverse = inverse32[...].astype(BF16)
    adjoint = adjoint32[...].astype(BF16)

    def parts(block):
        return block[:, :KB].astype(F32), block[:, KB:].astype(F32)

    grad_copies = []
    for slot in range(tiles):
        t = lax.rem(place + tiles - slot, tiles)
        start = pl.multiple_of(t * TS, TS)
        if slot > 0:
            kernel_copies[slot - 1].wait_recv()
        sre = scale * spec_ref[0, t].astype(F32)
        sim = scale * spec_ref[1, t].astype(F32)

        def forward(pair, carry):
            w = []
            for q in range(2):
                kr, ki = parts(held[slot, 2 * pair + q])
                w.append(((kr * sre + ki * sim).astype(BF16), (kr * sim - ki * sre).astype(BF16)))
            both = row_join([lane_join([w[0][h], w[1][h]]) for h in range(2)])
            turned = dot(turn, both).astype(BF16)
            for q in range(2):
                at = pl.ds(pl.multiple_of((2 * pair + q) * rows, rows), rows)
                lanes = slice(q * KB, (q + 1) * KB)
                wave_ref[at, :] = lane_join([turned[:rows, lanes], turned[rows:, lanes]])
            return carry

        lax.fori_loop(0, NR // 2, forward, 0, unroll=2)
        field_ref[...] = dot(wave_ref[...], inverse)

        def energy(k, total):
            field = field_ref[pl.ds(pl.multiple_of(k * rows, rows), rows), :]
            return total + field * field

        intensity = lax.fori_loop(0, NR, energy, jnp.zeros((rows, TS), F32), unroll=4)
        resist = 1.0 / (1.0 + jnp.exp(-STEEPNESS * (intensity - THRESHOLD)))
        goal = target_ref[:, pl.ds(start, TS)].astype(F32)
        resist_ref[:, pl.ds(start, TS)] = resist.astype(BF16)
        slope = 4.0 * (resist - goal) * STEEPNESS * resist * (1.0 - resist)

        def weigh(k, carry):
            at = pl.ds(pl.multiple_of(k * rows, rows), rows)
            wave_ref[at, :] = (field_ref[at, :] * slope).astype(BF16)
            return carry

        lax.fori_loop(0, NR, weigh, 0, unroll=4)
        wave_ref[...] = dot(wave_ref[...], adjoint).astype(BF16)

        def gather(pair, carry):
            acc_re, acc_im = carry
            waves = [
                wave_ref[pl.ds(pl.multiple_of((2 * pair + q) * rows, rows), rows), :]
                for q in range(2)
            ]
            both = row_join(
                [lane_join([waves[q][:, h * KB : (h + 1) * KB] for q in range(2)]) for h in range(2)]
            )
            turned = dot(back, both)
            for q in range(2):
                kr, ki = parts(held[slot, 2 * pair + q])
                tr = turned[:KB, q * KB : (q + 1) * KB]
                ti = turned[KB:, q * KB : (q + 1) * KB]
                acc_re = acc_re + kr * tr + ki * ti
                acc_im = acc_im + ki * tr - kr * ti
            return acc_re, acc_im

        zero = jnp.zeros((KB, KB), F32)
        acc_re, acc_im = lax.fori_loop(0, NR // 2, gather, (zero, zero), unroll=2)
        part_ref[slot, 0] = acc_re.astype(BF16)
        part_ref[slot, 1] = acc_im.astype(BF16)
        grad_copies.append(
            [
                send(
                    part_ref.at[slot], got_ref.at[slot, step], g_send.at[slot, step],
                    g_recv.at[slot, step], (peer, me),
                )
                for step, peer in enumerate(peers)
            ]
        )

    acc_ref[...] = jnp.zeros_like(acc_ref)
    spread = spread32[...].astype(BF16)
    for copies in grad_copies:
        for copy in copies:
            copy.wait_recv()
    for slot in range(tiles):
        t = lax.rem(place + tiles - slot, tiles)
        at = pl.ds(pl.multiple_of(t * TS, TS), TS + 2 * HALO)
        total = part_ref[slot].astype(F32)
        for step in range(1, group):
            total = total + got_ref[(slot - step) % tiles, step - 1].astype(F32)
        total = (scale * total).astype(BF16)
        rows_back = dot(turn, row_join([total[0], total[1]])).astype(BF16)
        patch = dot(lane_join([rows_back[:rows], rows_back[rows:]]), spread)
        acc_ref[:, at] = acc_ref[:, at] + patch

    width = tiles * TS
    lane = lax.broadcasted_iota(jnp.int32, (rows, 2 * HALO), 1)
    low = lane < HALO
    rim_ref[...] = jnp.where(
        low, acc_ref[:, : 2 * HALO], acc_ref[:, width : width + 2 * HALO]
    ).astype(BF16)
    rims = [
        send(rim_ref, left_ref, r_send.at[0], r_recv.at[0], (rank, right)),
        send(rim_ref, right_ref, r_send.at[1], r_recv.at[1], (rank, left)),
    ]
    inner = pltpu.roll(acc_ref[...], width + HALO, 1)[:, :width]
    rims[0].wait_recv()
    rims[1].wait_recv()
    from_left = pltpu.roll(left_ref[...].astype(F32), HALO, 1)
    from_right = pltpu.roll(right_ref[...].astype(F32), HALO, 1)
    from_left = jnp.where(low & (me > 0), from_left, 0.0)
    from_right = jnp.where((lane >= HALO) & (me < line - 1), from_right, 0.0)
    blocks = [
        inner[:, : 2 * HALO] + from_left,
        inner[:, 2 * HALO : width - 2 * HALO],
        inner[:, width - 2 * HALO :] + from_right,
    ]
    grad_ref[...] = lane_join(blocks).astype(BF16)
    for copy in kernel_copies + [c for copies in grad_copies for c in copies] + rims:
        copy.wait_send()


def image(own, spectra, target, scale):
    tiles = spectra.shape[1]
    rows = target.shape[0]
    group, line = lax.axis_size("src"), lax.axis_size("tile")
    tables = [jnp.asarray(t) for t in imaging_tables(group)]
    vmem = pl.BlockSpec(memory_space=pltpu.VMEM)
    hbm = pl.BlockSpec(memory_space=pl.ANY)
    dma = pltpu.SemaphoreType.DMA
    return pl.pallas_call(
        functools.partial(
            image_kernel, group=group, line=line, tiles=tiles, rows=rows, scale=scale
        ),
        out_shape=(
            jax.ShapeDtypeStruct(target.shape, BF16),
            jax.ShapeDtypeStruct(target.shape, BF16),
        ),
        in_specs=[hbm, vmem, vmem] + [hbm] * len(tables),
        out_specs=(vmem, vmem),
        scratch_shapes=[
            pltpu.VMEM((tiles,) + own.shape, BF16),
            pltpu.VMEM(tables[0].shape[1:], F32),
            pltpu.VMEM(tables[1].shape[1:], F32),
            pltpu.VMEM(tables[2].shape, F32),
            pltpu.VMEM(tables[3].shape, F32),
            pltpu.VMEM(tables[4].shape, F32),
            pltpu.VMEM((NR * rows, TS), BF16),
            pltpu.VMEM((NR * rows, TS), F32),
            pltpu.VMEM((tiles, 2, KB, KB), BF16),
            pltpu.VMEM((tiles, group - 1, 2, KB, KB), BF16),
            pltpu.VMEM((rows, tiles * TS + 2 * HALO), F32),
            pltpu.VMEM((rows, 2 * HALO), BF16),
            pltpu.VMEM((rows, 2 * HALO), BF16),
            pltpu.VMEM((rows, 2 * HALO), BF16),
            dma((6,)),
            dma((tiles,)),
            dma((tiles,)),
            dma((tiles, group - 1)),
            dma((tiles, group - 1)),
            dma((2,)),
            dma((2,)),
        ],
        compiler_params=pltpu.CompilerParams(
            vmem_limit_bytes=56 * 2**20, collective_id=0, has_side_effects=True
        ),
        cost_estimate=pl.CostEstimate(
            flops=2 * 10**9, bytes_accessed=4 * 10**6, transcendentals=0
        ),
    )(own, spectra, target, *tables)


def on_device(mask, target, start_block, zernike, source_points, source_weight, tile_slit):
    rank = lax.axis_index("src")
    rows_here = mask.shape[0]
    tiles_here = tile_slit.shape[0]
    patch_width = TS + 2 * HALO
    spectrum_scale = 1.0 / math.sqrt(TS * patch_width)
    extended = with_halo(mask, (("tile", 1),), HALO)
    cosine, sine, column_cos, column_sin = phase_tables()
    row_table = lax.dynamic_slice_in_dim(
        jnp.asarray(np.concatenate([cosine, sine], axis=1)), rank * rows_here, rows_here, 0
    )
    column_forward = jnp.asarray(np.concatenate([column_cos, -column_sin], axis=1))
    patches = jnp.stack(
        [extended[:, counter * TS : counter * TS + patch_width] for counter in range(tiles_here)]
    )
    columns = jnp.einsum(
        "jxy,yc->jxc", patches, column_forward, preferred_element_type=jnp.float32
    ).astype(jnp.bfloat16)
    row_sums = jnp.einsum("xc,jxd->jcd", row_table, columns, preferred_element_type=jnp.float32)
    partial_re = row_sums[:, :KB, :KB] + row_sums[:, KB:, KB:]
    partial_im = row_sums[:, :KB, KB:] - row_sums[:, KB:, :KB]
    partial = jnp.stack([partial_re, partial_im]).astype(jnp.bfloat16)
    slit = lax.dynamic_slice_in_dim(tile_slit, rank % tiles_here, 1, 0)
    partial, slit = lax.optimization_barrier((partial, slit))
    spectra = lax.psum(partial, "src")
    own = synthesize(slit, zernike, start_block, source_points, source_weight)
    return image(own, spectra, target, spectrum_scale)


def solution(mesh):
    placed = (P("src", "tile"), P("src", "tile"), P(), P(), P(), P(), P("tile"))
    return jax.shard_map(
        on_device,
        mesh=mesh,
        in_specs=placed,
        out_specs=(P("src", "tile"), P("src", "tile")),
        check_vma=False,
    )
```

```python
import functools
import math

import jax
import jax.numpy as jnp
import ml_dtypes
import numpy as np
from jax import lax
from jax.experimental import pallas as pl
from jax.experimental.pallas import tpu as pltpu
from jax.sharding import PartitionSpec as P

KB = 128
NR = 24
NZ = 37
RAD = 40
SHIFT = 24
HALO = 64
ITERS = 4
TS = 256
LAGS = 2 * SHIFT + 1
LP = 64
DISC = 88

STEEPNESS = 4.0
THRESHOLD = 0.5
RIDGE_SHARE = 0.001
F32 = jnp.float32
BF16 = jnp.bfloat16


def noll_terms(term_count):
    listing = []
    degree = 0
    while len(listing) < term_count:
        for azimuth in range(degree % 2, degree + 1, 2):
            if azimuth == 0:
                listing.append((degree, 0, 0))
            else:
                for repeat in range(2):
                    number = len(listing) + 1
                    listing.append((degree, azimuth, 2 if number % 2 == 0 else 1))
        degree += 1
    return listing[:term_count]


def radial_terms(degree, azimuth):
    powers = []
    for counter in range((degree - azimuth) // 2 + 1):
        factor = (
            (-1) ** counter
            * math.factorial(degree - counter)
            / (
                math.factorial(counter)
                * math.factorial((degree + azimuth) // 2 - counter)
                * math.factorial((degree - azimuth) // 2 - counter)
            )
        )
        powers.append((degree - 2 * counter, factor))
    return powers


@functools.lru_cache(None)
def zernike_table():
    u = (np.arange(DISC) - RAD)[:, None]
    v = (np.arange(KB) - RAD)[None, :]
    inside = (u * u + v * v <= RAD * RAD).astype(np.float64)
    rho = np.sqrt(u * u + v * v) / RAD
    theta = np.arctan2(v + 0.0 * u, u + 0.0 * v)
    planes = []
    for degree, azimuth, parity in noll_terms(NZ):
        radial = sum(f * rho**e for e, f in radial_terms(degree, azimuth))
        if azimuth == 0:
            plane = math.sqrt(degree + 1.0) * radial
        else:
            turn = np.cos if parity == 2 else np.sin
            plane = math.sqrt(2.0 * degree + 2.0) * radial * turn(azimuth * theta)
        planes.append(plane * inside)
    planes.append(inside)
    return np.stack(planes).astype(np.float32)


@functools.lru_cache(None)
def dft_tables():
    f = np.arange(KB)
    angle = 2.0 * np.pi / KB * ((f[:, None] * f[None, :]) % KB)
    return np.cos(angle).astype(np.float32), np.sin(angle).astype(np.float32)


def halves(x):
    high = x.astype(BF16)
    return high, (x - high.astype(F32)).astype(BF16)


def dot(x, y):
    return jnp.dot(x.astype(BF16), y.astype(BF16), preferred_element_type=F32)


def nt_mul(x, y):
    xh, xl = halves(x)
    yh, yl = halves(y)
    dims = (((1,), (1,)), ((), ()))
    return (
        lax.dot_general(xh, yh, dims, preferred_element_type=F32)
        + lax.dot_general(xl, yh, dims, preferred_element_type=F32)
        + lax.dot_general(xh, yl, dims, preferred_element_type=F32)
    )


def small_mul(m, x):
    mh, ml = halves(m)
    xh, xl = halves(x)
    return (
        jnp.dot(mh, xh, preferred_element_type=F32)
        + jnp.dot(ml, xh, preferred_element_type=F32)
        + jnp.dot(mh, xl, preferred_element_type=F32)
    )


def exact_dot(x, y):
    xh, xl = halves(x)
    yh, yl = halves(y)
    return dot(xh, yh) + dot(xl, yh) + dot(xh, yl)


def lane_join(parts):
    return jnp.concatenate(parts, axis=1)


def row_join(parts):
    return jnp.concatenate(parts, axis=0)


def eliminate(gram, floor):
    row = lax.broadcasted_iota(jnp.int32, (NR, KB), 0)
    lane = lax.broadcasted_iota(jnp.int32, (NR, KB), 1)
    aug = lane_join([gram, jnp.zeros((NR, KB - NR), F32)])
    aug = aug + jnp.where(lane == row + NR, 1.0, 0.0)
    scales = jnp.zeros((NR, KB), F32)
    block = 4
    for begin in range(0, NR, block):
        cols = [
            jnp.broadcast_to(aug[:, j : j + 1], (NR, KB)) for j in range(begin, begin + block)
        ]
        for m in range(block):
            j = begin + m
            pivot = cols[m][j : j + 1, :]
            good = pivot > floor
            safe = jnp.where(good, pivot, 1.0)
            inverse = jnp.where(good, 1.0 / safe, 0.0)
            root = jnp.where(good, lax.rsqrt(safe), 0.0)
            factor = jnp.where(row > j, cols[m] * inverse, 0.0)
            aug = aug - factor * aug[j : j + 1, :]
            for later in range(m + 1, block):
                cols[later] = cols[later] - factor * cols[later][j : j + 1, :]
            scales = jnp.where(row == j, root, scales)
    return aug * scales


GROUP = 8


@functools.lru_cache(None)
def phase_tables():
    frequency = np.arange(KB) - KB // 2

    def make(period):
        angle = 2.0 * np.pi / period * np.mod(np.arange(period)[:, None] * frequency, period)
        return [
            turn(angle.astype(np.float32)).astype(ml_dtypes.bfloat16) for turn in (np.cos, np.sin)
        ]

    return make(TS) + make(TS + 2 * HALO)


@functools.lru_cache(None)
def imaging_tables(group):
    cosine, sine, column_cos, column_sin = [t.astype(np.float32) for t in phase_tables()]
    rows = TS // group
    turns, backs = [], []
    for rank in range(group):
        c, s = [t[rank * rows : (rank + 1) * rows] for t in (cosine, sine)]
        turns.append(np.block([[c, -s], [s, c]]))
        backs.append(np.block([[c.T, -s.T], [s.T, c.T]]))
    inner = slice(HALO, HALO + TS)
    inverse = np.concatenate([column_cos[inner], -column_sin[inner]], axis=1).T
    adjoint = np.concatenate([column_cos[inner], column_sin[inner]], axis=1)
    spread = np.concatenate([column_cos, -column_sin], axis=1).T
    return tuple(
        np.ascontiguousarray(t) for t in (np.stack(turns), np.stack(backs), inverse, adjoint, spread)
    )


def whole_kernel(
    slit_ref, zern_ref, points_ref, weight_ref, mask_ref, target_ref,
    basis_hbm, cos_hbm, sin_hbm, block_hbm, back_hbm, spread_hbm, turn_hbm, inverse_hbm, adjoint_hbm,
    resist_ref, grad_ref,
    basis_ref, cos_ref, sin_ref, block_ref, back32_ref, spread32, turn32, inverse32, adjoint32,
    full, full_back, lag, lag_back,
    y_ref, z_ref, power_ref, pre_ref, pim_ref, edge_ref,
    held, wave_ref, field_ref, part_ref, got_ref, spart_ref, sgot_ref,
    acc_ref, rim_ref, left_ref, right_ref, mask_left, mask_right,
    local_sems, k_send, k_recv, g_send, g_recv, s_send, s_recv, r_send, r_recv, h_send, h_recv,
    *, group, line, tiles, rows, scale,
):
    rank, me = lax.axis_index("src"), lax.axis_index("tile")
    place = lax.rem(rank, tiles)
    right = lax.rem(me + 1, line)
    left = lax.rem(me + line - 1, line)
    peers = [lax.rem(rank + step, group) for step in range(1, group)]
    barrier = pltpu.get_barrier_semaphore()
    for peer in peers:
        pl.semaphore_signal(
            barrier, inc=1, device_id=(peer, me), device_id_type=pl.DeviceIdType.MESH
        )
    for side in (left, right):
        pl.semaphore_signal(
            barrier, inc=1, device_id=(rank, side), device_id_type=pl.DeviceIdType.MESH
        )
    loads = [
        (basis_hbm, basis_ref), (cos_hbm, cos_ref), (sin_hbm, sin_ref), (block_hbm, block_ref),
        (back_hbm.at[rank], back32_ref), (spread_hbm, spread32), (turn_hbm.at[rank], turn32),
        (inverse_hbm, inverse32), (adjoint_hbm, adjoint32),
    ]
    copies = [pltpu.make_async_copy(a, b, local_sems.at[i]) for i, (a, b) in enumerate(loads)]
    for copy in copies:
        copy.start()
    width = tiles * TS

    def send(src, dst, send_sem, recv_sem, device):
        copy = pltpu.make_async_remote_copy(
            src_ref=src, dst_ref=dst, send_sem=send_sem, recv_sem=recv_sem,
            device_id=device, device_id_type=pl.DeviceIdType.MESH,
        )
        copy.start()
        return copy

    halo_copies, spectrum_copies, kernel_copies = [], [], []

    def begin_exchange():
        pl.semaphore_wait(barrier, group - 1 + 2)
        ends = (mask_ref.at[:, width - 2 * HALO :], mask_ref.at[:, : 2 * HALO])
        halo_copies.append(send(ends[0], mask_left, h_send.at[0], h_recv.at[0], (rank, right)))
        halo_copies.append(send(ends[1], mask_right, h_send.at[1], h_recv.at[1], (rank, left)))

    def send_spectra():
        for copy in halo_copies:
            copy.wait_recv()
        for copy in copies[4:6]:
            copy.wait()
        spread = spread32[...].astype(BF16)
        back = back32_ref[...].astype(BF16)
        before = jnp.where(me > 0, mask_left[...].astype(F32), 0.0)
        after = jnp.where(me < line - 1, mask_right[...].astype(F32), 0.0)
        wide = lane_join([before, mask_ref[...].astype(F32), after])
        wide = pltpu.roll(wide, width + 3 * HALO, 1)
        for t in range(tiles):
            patch = wide[:, t * TS : (t + 1) * TS + 2 * HALO].astype(BF16)
            columns = lax.dot_general(
                patch, spread, (((1,), (1,)), ((), ())), preferred_element_type=F32
            ).astype(BF16)
            sums = dot(back, row_join([columns[:, :KB], -columns[:, KB:]]))
            spart_ref[t, 0] = sums[:KB].astype(BF16)
            spart_ref[t, 1] = (-sums[KB:]).astype(BF16)
        for step, peer in enumerate(peers):
            spectrum_copies.append(
                send(spart_ref, sgot_ref.at[step], s_send.at[step], s_recv.at[step], (peer, me))
            )

    lane = lax.broadcasted_iota(jnp.int32, (1, KB), 1)
    total = jnp.sum(weight_ref[...], axis=1, keepdims=True)
    weight = weight_ref[...] / (math.pi * RAD * RAD * total)
    px = SHIFT - points_ref[:, 0:1]
    py = SHIFT - points_ref[:, 1:2]
    lag_lane = lax.broadcasted_iota(jnp.int32, (points_ref.shape[0], KB), 1)
    hot_x = jnp.where(lag_lane == px, 1.0, 0.0).T[:LP]
    hot_y = jnp.where(jnp.where(lag_lane < LP, lag_lane, lag_lane - LP) == py, 1.0, 0.0)
    high, low = halves(hot_x * weight)
    omega = dot(high, hot_y) + dot(low, hot_y)
    omega_cat = lane_join([omega[i : i + 1] for i in range(LAGS)])
    begin_exchange()
    copies[0].wait()
    slit = slit_ref[place]
    waves = zern_ref[slit, 0] * basis_ref[0]
    for z in range(1, NZ):
        waves = waves + zern_ref[slit, z] * basis_ref[z]
    inside = basis_ref[NZ]
    angle = 2.0 * math.pi * waves
    pr = inside * jnp.cos(angle)
    pi = inside * jnp.sin(angle)
    p40 = (pr[80:81, 40:41], pi[80:81, 40:41])
    m40 = (pr[0:1, 40:41], pi[0:1, 40:41])
    q40 = (pr[40:41, 80:81], pi[40:41, 80:81])
    n40 = (pr[40:41, 0:1], pi[40:41, 0:1])
    for copy in copies[1:3]:
        copy.wait()
    c, s = cos_ref[...], sin_ref[...]
    full32 = row_join([lane_join([c, -s]), lane_join([s, c])])
    back32 = row_join([lane_join([c, s]), lane_join([-s, c])])
    full[...] = full32.astype(BF16)
    full_back[...] = back32.astype(BF16)
    keep_row = lax.broadcasted_iota(jnp.int32, (LP, KB), 0) < LAGS
    cy, sy = jnp.where(keep_row, c[:LP], 0.0), jnp.where(keep_row, s[:LP], 0.0)
    lag[...] = row_join([lane_join([cy, -sy]), lane_join([sy, cy])]).astype(BF16)
    keep_lane = lax.broadcasted_iota(jnp.int32, (KB, KB), 1) < LAGS
    ct, st = jnp.where(keep_lane, c, 0.0), jnp.where(keep_lane, s, 0.0)
    lag_back[...] = row_join(
        [ct + pltpu.roll(st, LP, 1), pltpu.roll(ct, LP, 1) - st]
    ).astype(BF16)
    pupil = row_join([lane_join([pr, pi]), jnp.zeros((KB - DISC, 2 * KB), F32)])
    half = exact_dot(pupil, full32)
    hat = exact_dot(back32, row_join([half[:, :KB], half[:, KB:]]))
    hat = (hat[:KB], hat[KB:])
    unit = 1.0 / (KB * KB)
    pre_ref[...] = unit * hat[0]
    pim_ref[...] = unit * hat[1]
    power_ref[...] = unit * (hat[0] * hat[0] + hat[1] * hat[1])
    send_spectra()

    def times(scalar, re, im, conj):
        a, b = scalar
        b = -b if conj else b
        return a * re - b * im, a * im + b * re

    def entries(shape, items):
        row = lax.broadcasted_iota(jnp.int32, shape, 0)
        col = lax.broadcasted_iota(jnp.int32, shape, 1)
        matrix = jnp.zeros(shape, F32)
        for i, j, value in items:
            matrix = matrix + jnp.where((row == i) & (col == j), value, 0.0)
        return matrix.astype(BF16)

    end = LAGS - 1
    qr, qi = q40
    ar, ai = times(n40, qr, qi, True)
    start_fix = entries(
        (2 * KB, KB),
        [(0, end, -qr), (KB, end, -qi), (0, LP + end, qi), (KB, LP + end, -qr)],
    )
    gram_fix = entries(
        (KB, KB),
        [
            (end, 0, -ar), (LP + end, 0, ai), (LP + end, LP, -ar), (end, LP, -ai),
            (end, end, -1.0), (0, end, -ar), (LP, end, -ai),
            (LP + end, LP + end, -1.0), (LP, LP + end, -ar), (0, LP + end, ai),
        ],
    )
    final_fix = entries(
        (KB, 2 * KB),
        [(end, 0, -qr), (LP + end, 0, qi), (end, KB, -qi), (LP + end, KB, -qr)],
    )

    copies[3].wait()

    def lanes_of(x, g):
        return x[:, g * KB : (g + 1) * KB]

    def stack(x, rows):
        x = x.astype(BF16)
        pieces = [x[g * rows : (g + 1) * rows] for g in range(GROUP)]
        return row_join(
            [lane_join([p[:, :KB] for p in pieces]), lane_join([p[:, KB:] for p in pieces])]
        )

    def unstack(x):
        x = x.astype(BF16)
        rows = x.shape[0] // 2
        return row_join(
            [lane_join([lanes_of(x[:rows], g), lanes_of(x[rows:], g)]) for g in range(GROUP)]
        )

    def scaled(x, re, im):
        tops, lows = [], []
        for g in range(GROUP):
            hr, hi = lanes_of(x[:KB], g), lanes_of(x[KB:], g)
            if im is None:
                tops.append((re * hr).astype(BF16))
                lows.append((re * hi).astype(BF16))
            else:
                tops.append((re * hr - im * hi).astype(BF16))
                lows.append((re * hi + im * hr).astype(BF16))
        return row_join([lane_join(tops), lane_join(lows)])

    def start(group, carry):
        base = group * GROUP
        xs = [
            lane_join([block_ref[0, base + g].astype(BF16), block_ref[1, base + g].astype(BF16)])
            for g in range(GROUP)
        ]
        two = dot(full_back[...], stack(dot(row_join(xs), full[...]), KB))
        three = dot(lag[...], scaled(two, pre_ref[...], -pim_ref[...]))
        rims = row_join([x.astype(F32)[40 : 40 + LP].astype(BF16) for x in xs])
        c = dot(lane_join([unstack(three), rims]), row_join([lag_back[...], start_fix]))
        z_ref[pl.ds(pl.multiple_of(base * LP, GROUP * LP), GROUP * LP), :] = c
        return carry

    lax.fori_loop(0, NR // GROUP, start, 0)
    at_first = pl.ds(0, NR, stride=LP)
    at_last = pl.ds(end, NR, stride=LP)
    within = lane < LAGS
    er = row_join([block_ref[0, k, 0:1, :] for k in range(NR)])
    ei = row_join([block_ref[1, k, 0:1, :] for k in range(NR)])
    er = jnp.where(within, pltpu.roll(er, KB - 40, 1), 0.0)
    ei = jnp.where(within, pltpu.roll(ei, KB - 40, 1), 0.0)
    er, ei = times(p40, er, ei, True)
    z_ref[at_last, :] = z_ref[at_last, :] - (er + pltpu.roll(ei, LP, 1))

    def load_cat(ref):
        return lane_join([ref[pl.ds(i, NR, stride=LP), :] for i in range(LAGS)])

    def store_cat(ref, value):
        for i in range(LAGS):
            ref[pl.ds(i, NR, stride=LP), :] = value[:, i * KB : (i + 1) * KB]

    y_ref[...] = jnp.zeros_like(y_ref)
    store_cat(y_ref, load_cat(z_ref) * omega_cat)

    def turned(scalar_a, scalar_b, value):
        cr, ci = times(scalar_a, scalar_b[0], scalar_b[1], True)
        return cr * value + jnp.where(lane < LP, -ci, ci) * pltpu.roll(value, LP, 1)

    def apply_gram():
        def body(group, carry):
            base = pl.multiple_of(group * GROUP * LP, GROUP * LP)
            at = pl.ds(base, GROUP * LP)
            y = y_ref[at, :].astype(BF16)
            two = dot(lag_back[...], stack(dot(y, lag[...]), LP))
            three = dot(lag[...], scaled(two, power_ref[...], None))
            z_ref[at, :] = dot(
                lane_join([unstack(three), y]), row_join([lag_back[...], gram_fix])
            )
            return carry

        lax.fori_loop(0, NR // GROUP, body, 0)
        y_first, y_last = y_ref[at_first, :], y_ref[at_last, :]
        z_ref[at_first, :] = z_ref[at_first, :] - turned(m40, p40, y_last)
        z_ref[at_last, :] = z_ref[at_last, :] - (y_last + turned(p40, m40, y_first))

    eye = lax.broadcasted_iota(jnp.int32, (NR, NR), 0) == lax.broadcasted_iota(
        jnp.int32, (NR, NR), 1
    )

    def trace_of(m):
        return jnp.sum(
            jnp.sum(jnp.where(eye, m, 0.0), axis=1, keepdims=True), axis=0, keepdims=True
        )

    for it in range(ITERS):
        apply_gram()
        yc, zc = load_cat(y_ref), load_cat(z_ref)
        gram = nt_mul(yc, zc)
        ridge = RIDGE_SHARE * trace_of(gram) / NR + 1e-06
        gram = gram + jnp.where(eye, ridge, 0.0)
        inverse = eliminate(gram, 0.0)[:, NR : 2 * NR]
        projected = small_mul(inverse, zc)
        if it < ITERS - 1:
            store_cat(y_ref, projected * omega_cat)
        else:
            mixing = nt_mul(projected * omega_cat, projected)
            upper = eliminate(mixing, 1e-6 * trace_of(mixing))[:, :NR]
            store_cat(y_ref, small_mul(small_mul(upper, inverse), yc))

    last = y_ref[at_last, :]
    er = pltpu.roll(jnp.where(lane < LP, last, 0.0), 40, 1)
    ei = pltpu.roll(jnp.where(lane < LP, 0.0, last), 40 + LP, 1)
    er, ei = times(p40, er, ei, False)
    edge_ref[...] = lane_join([er, ei])

    for group_index in range(NR // GROUP):
        base = group_index * GROUP
        y = y_ref[base * LP : (base + GROUP) * LP, :].astype(BF16)
        two = dot(lag_back[...], stack(dot(y, lag[...]), LP))
        three = dot(full[...], scaled(two, pre_ref[...], pim_ref[...]))
        a = dot(unstack(three), full_back[...])
        fix = dot(y, final_fix)
        edges = edge_ref[base : base + GROUP, :]
        for g in range(GROUP):
            top = g * KB
            head = a[top : top + 8]
            first_row = lax.broadcasted_iota(jnp.int32, head.shape, 0) == 0
            head = head - jnp.where(first_row, edges[g : g + 1], 0.0)
            held[0, base + g] = row_join(
                [
                    head,
                    a[top + 8 : top + 40],
                    a[top + 40 : top + 40 + LP] + fix[g * LP : (g + 1) * LP],
                    a[top + 40 + LP : top + KB],
                ]
            ).astype(BF16)
        span = pl.ds(base, GROUP)
        for step in range(1, tiles):
            kernel_copies.append(
                send(
                    held.at[0, span], held.at[step, span], k_send.at[step - 1, group_index],
                    k_recv.at[step - 1, group_index],
                    (rank - place + lax.rem(place + step, tiles), me),
                )
            )

    copies[6].wait()
    turn = turn32[...].astype(BF16)
    back = back32_ref[...].astype(BF16)
    spread = spread32[...].astype(BF16)
    for load in copies[7:]:
        load.wait()
    inverse = inverse32[...].astype(BF16)
    adjoint = adjoint32[...].astype(BF16)

    def parts(block):
        return block[:, :KB].astype(F32), block[:, KB:].astype(F32)

    for copy in spectrum_copies:
        copy.wait_recv()
    grad_copies = []
    for slot in range(tiles):
        t = lax.rem(place + tiles - slot, tiles)
        start = pl.multiple_of(t * TS, TS)
        if slot > 0:
            for copy in kernel_copies[slot - 1 :: tiles - 1]:
                copy.wait_recv()
        spectrum = spart_ref[t].astype(F32)
        for step in range(group - 1):
            spectrum = spectrum + sgot_ref[step, t].astype(F32)
        sre, sim = scale * spectrum[0], scale * spectrum[1]

        def forward(pair, carry):
            w = []
            for q in range(2):
                kr, ki = parts(held[slot, 2 * pair + q])
                w.append(((kr * sre + ki * sim).astype(BF16), (kr * sim - ki * sre).astype(BF16)))
            both = row_join([lane_join([w[0][h], w[1][h]]) for h in range(2)])
            turned = dot(turn, both).astype(BF16)
            for q in range(2):
                at = pl.ds(pl.multiple_of((2 * pair + q) * rows, rows), rows)
                lanes = slice(q * KB, (q + 1) * KB)
                wave_ref[at, :] = lane_join([turned[:rows, lanes], turned[rows:, lanes]])
            return carry

        lax.fori_loop(0, NR // 2, forward, 0, unroll=2)
        field_ref[...] = dot(wave_ref[...], inverse)

        def energy(k, total):
            field = field_ref[pl.ds(pl.multiple_of(k * rows, rows), rows), :]
            return total + field * field

        intensity = lax.fori_loop(0, NR, energy, jnp.zeros((rows, TS), F32), unroll=4)
        resist = 1.0 / (1.0 + jnp.exp(-STEEPNESS * (intensity - THRESHOLD)))
        goal = target_ref[:, pl.ds(start, TS)].astype(F32)
        resist_ref[:, pl.ds(start, TS)] = resist.astype(BF16)
        slope = 4.0 * (resist - goal) * STEEPNESS * resist * (1.0 - resist)

        def weigh(k, carry):
            at = pl.ds(pl.multiple_of(k * rows, rows), rows)
            wave_ref[at, :] = (field_ref[at, :] * slope).astype(BF16)
            return carry

        lax.fori_loop(0, NR, weigh, 0, unroll=4)
        wave_ref[...] = dot(wave_ref[...], adjoint).astype(BF16)

        def gather(pair, carry):
            acc_re, acc_im = carry
            waves = [
                wave_ref[pl.ds(pl.multiple_of((2 * pair + q) * rows, rows), rows), :]
                for q in range(2)
            ]
            both = row_join(
                [lane_join([waves[q][:, h * KB : (h + 1) * KB] for q in range(2)]) for h in range(2)]
            )
            turned = dot(back, both)
            for q in range(2):
                kr, ki = parts(held[slot, 2 * pair + q])
                tr = turned[:KB, q * KB : (q + 1) * KB]
                ti = turned[KB:, q * KB : (q + 1) * KB]
                acc_re = acc_re + kr * tr + ki * ti
                acc_im = acc_im + ki * tr - kr * ti
            return acc_re, acc_im

        zero = jnp.zeros((KB, KB), F32)
        acc_re, acc_im = lax.fori_loop(0, NR // 2, gather, (zero, zero), unroll=2)
        part_ref[slot, 0] = acc_re.astype(BF16)
        part_ref[slot, 1] = acc_im.astype(BF16)
        grad_copies.append(
            [
                send(
                    part_ref.at[slot], got_ref.at[slot, step], g_send.at[slot, step],
                    g_recv.at[slot, step], (peer, me),
                )
                for step, peer in enumerate(peers)
            ]
        )

    acc_ref[...] = jnp.zeros_like(acc_ref)
    for copies in grad_copies:
        for copy in copies:
            copy.wait_recv()
    for slot in range(tiles):
        t = lax.rem(place + tiles - slot, tiles)
        at = pl.ds(pl.multiple_of(t * TS, TS), TS + 2 * HALO)
        total = part_ref[slot].astype(F32)
        for step in range(1, group):
            total = total + got_ref[(slot - step) % tiles, step - 1].astype(F32)
        total = (scale * total).astype(BF16)
        rows_back = dot(turn, row_join([total[0], total[1]])).astype(BF16)
        patch = dot(lane_join([rows_back[:rows], rows_back[rows:]]), spread)
        acc_ref[:, at] = acc_ref[:, at] + patch

    lane = lax.broadcasted_iota(jnp.int32, (rows, 2 * HALO), 1)
    low = lane < HALO
    rim_ref[...] = jnp.where(
        low, acc_ref[:, : 2 * HALO], acc_ref[:, width : width + 2 * HALO]
    ).astype(BF16)
    rims = [
        send(rim_ref, left_ref, r_send.at[0], r_recv.at[0], (rank, right)),
        send(rim_ref, right_ref, r_send.at[1], r_recv.at[1], (rank, left)),
    ]
    inner = pltpu.roll(acc_ref[...], width + HALO, 1)[:, :width]
    rims[0].wait_recv()
    rims[1].wait_recv()
    from_left = pltpu.roll(left_ref[...].astype(F32), HALO, 1)
    from_right = pltpu.roll(right_ref[...].astype(F32), HALO, 1)
    from_left = jnp.where(low & (me > 0), from_left, 0.0)
    from_right = jnp.where((lane >= HALO) & (me < line - 1), from_right, 0.0)
    blocks = [
        inner[:, : 2 * HALO] + from_left,
        inner[:, 2 * HALO : width - 2 * HALO],
        inner[:, width - 2 * HALO :] + from_right,
    ]
    grad_ref[...] = lane_join(blocks).astype(BF16)
    for copy in halo_copies + spectrum_copies + kernel_copies + [c for copies in grad_copies for c in copies] + rims:
        copy.wait_send()


def on_device(mask, target, start_block, zernike, source_points, source_weight, tile_slit):
    tiles = tile_slit.shape[0]
    rows = mask.shape[0]
    group, line = lax.axis_size("src"), lax.axis_size("tile")
    scale = 1.0 / math.sqrt(TS * (TS + 2 * HALO))
    turns, backs, inverse, adjoint, spread = imaging_tables(group)
    cosine, sine = dft_tables()
    held = [
        jnp.asarray(t)
        for t in (zernike_table(), cosine, sine, start_block, backs, spread, turns, inverse, adjoint)
    ]
    vmem = pl.BlockSpec(memory_space=pltpu.VMEM)
    smem = pl.BlockSpec(memory_space=pltpu.SMEM)
    hbm = pl.BlockSpec(memory_space=pl.ANY)
    dma = pltpu.SemaphoreType.DMA
    own = [x.shape[1:] if x.shape[0] == group and x.ndim == 3 else x.shape for x in held]
    steps = group - 1
    scratch = [pltpu.VMEM(shape, F32) for shape in own]
    scratch += [
        pltpu.VMEM(shape, BF16)
        for shape in [(2 * KB, 2 * KB), (2 * KB, 2 * KB), (KB, 2 * KB), (2 * KB, KB)]
    ]
    scratch += [
        pltpu.VMEM(shape, F32)
        for shape in [(NR * LP, KB), (NR * LP, KB), (KB, KB), (KB, KB), (KB, KB), (NR, 2 * KB)]
    ]
    scratch += [
        pltpu.VMEM((tiles, NR, KB, 2 * KB), BF16),
        pltpu.VMEM((NR * rows, TS), BF16),
        pltpu.VMEM((NR * rows, TS), F32),
        pltpu.VMEM((tiles, 2, KB, KB), BF16),
        pltpu.VMEM((tiles, steps, 2, KB, KB), BF16),
        pltpu.VMEM((tiles, 2, KB, KB), BF16),
        pltpu.VMEM((steps, tiles, 2, KB, KB), BF16),
        pltpu.VMEM((rows, tiles * TS + 2 * HALO), F32),
    ]
    scratch += [pltpu.VMEM((rows, 2 * HALO), BF16)] * 5
    scratch += [
        dma((len(held),)), dma((tiles, NR // GROUP)), dma((tiles, NR // GROUP)),
        dma((tiles, steps)), dma((tiles, steps)), dma((steps,)), dma((steps,)),
        dma((2,)), dma((2,)), dma((2,)), dma((2,)),
    ]
    return pl.pallas_call(
        functools.partial(
            whole_kernel, group=group, line=line, tiles=tiles, rows=rows, scale=scale
        ),
        out_shape=(
            jax.ShapeDtypeStruct(target.shape, BF16),
            jax.ShapeDtypeStruct(target.shape, BF16),
        ),
        in_specs=[smem, smem] + [vmem] * 4 + [hbm] * len(held),
        out_specs=(vmem, vmem),
        scratch_shapes=scratch,
        compiler_params=pltpu.CompilerParams(
            vmem_limit_bytes=56 * 2**20, collective_id=0, has_side_effects=True
        ),
        cost_estimate=pl.CostEstimate(
            flops=8 * 10**9, bytes_accessed=8 * 10**6, transcendentals=0
        ),
    )(tile_slit, zernike, source_points, source_weight[None, :], mask, target, *held)


def solution(mesh):
    placed = (P("src", "tile"), P("src", "tile"), P(), P(), P(), P(), P("tile"))
    return jax.shard_map(
        on_device,
        mesh=mesh,
        in_specs=placed,
        out_specs=(P("src", "tile"), P("src", "tile")),
        check_vma=False,
    )
```

```python
import functools
import math

import jax
import jax.numpy as jnp
import ml_dtypes
import numpy as np
from jax import lax
from jax.experimental import pallas as pl
from jax.experimental.pallas import tpu as pltpu
from jax.sharding import PartitionSpec as P

KB = 128
NR = 24
NZ = 37
RAD = 40
SHIFT = 24
HALO = 64
ITERS = 4
TS = 256
LAGS = 2 * SHIFT + 1
LP = 64
DISC = 88

STEEPNESS = 4.0
THRESHOLD = 0.5
RIDGE_SHARE = 0.001
F32 = jnp.float32
BF16 = jnp.bfloat16


def noll_terms(term_count):
    listing = []
    degree = 0
    while len(listing) < term_count:
        for azimuth in range(degree % 2, degree + 1, 2):
            if azimuth == 0:
                listing.append((degree, 0, 0))
            else:
                for repeat in range(2):
                    number = len(listing) + 1
                    listing.append((degree, azimuth, 2 if number % 2 == 0 else 1))
        degree += 1
    return listing[:term_count]


def radial_terms(degree, azimuth):
    powers = []
    for counter in range((degree - azimuth) // 2 + 1):
        factor = (
            (-1) ** counter
            * math.factorial(degree - counter)
            / (
                math.factorial(counter)
                * math.factorial((degree + azimuth) // 2 - counter)
                * math.factorial((degree - azimuth) // 2 - counter)
            )
        )
        powers.append((degree - 2 * counter, factor))
    return powers


@functools.lru_cache(None)
def zernike_table():
    u = (np.arange(DISC) - RAD)[:, None]
    v = (np.arange(KB) - RAD)[None, :]
    inside = (u * u + v * v <= RAD * RAD).astype(np.float64)
    rho = np.sqrt(u * u + v * v) / RAD
    theta = np.arctan2(v + 0.0 * u, u + 0.0 * v)
    planes = []
    for degree, azimuth, parity in noll_terms(NZ):
        radial = sum(f * rho**e for e, f in radial_terms(degree, azimuth))
        if azimuth == 0:
            plane = math.sqrt(degree + 1.0) * radial
        else:
            turn = np.cos if parity == 2 else np.sin
            plane = math.sqrt(2.0 * degree + 2.0) * radial * turn(azimuth * theta)
        planes.append(plane * inside)
    planes.append(inside)
    return np.stack(planes).astype(np.float32)


@functools.lru_cache(None)
def dft_tables():
    f = np.arange(KB)
    angle = 2.0 * np.pi / KB * ((f[:, None] * f[None, :]) % KB)
    return np.cos(angle).astype(np.float32), np.sin(angle).astype(np.float32)


def halves(x):
    high = x.astype(BF16)
    return high, (x - high.astype(F32)).astype(BF16)


def dot(x, y):
    return jnp.dot(x.astype(BF16), y.astype(BF16), preferred_element_type=F32)


def split(x):
    high = x.astype(BF16).astype(F32)
    return high, x - high


def nt_mul(x, y):
    n, m = x.shape[0], y.shape[0]
    left = jnp.concatenate(split(x), axis=0).astype(BF16)
    right = jnp.concatenate(split(y), axis=0).astype(BF16)
    out = lax.dot_general(left, right, (((1,), (1,)), ((), ())), preferred_element_type=F32)
    return out[:n, :m] + out[n:, :m] + out[:n, m:]


def small_mul(m, x):
    mh, ml = split(m)
    xh, xl = split(x)
    return dot(lane_join([mh, mh, ml]), row_join([xh, xl, xh]))


def exact_dot(x, y):
    xh, xl = halves(x)
    yh, yl = halves(y)
    return dot(xh, yh) + dot(xl, yh) + dot(xh, yl)


def lane_join(parts):
    return jnp.concatenate(parts, axis=1)


def row_join(parts):
    return jnp.concatenate(parts, axis=0)


def eliminate(gram, floor):
    row = lax.broadcasted_iota(jnp.int32, (NR, KB), 0)
    lane = lax.broadcasted_iota(jnp.int32, (NR, KB), 1)
    aug = lane_join([gram, jnp.zeros((NR, KB - NR), F32)])
    aug = aug + jnp.where(lane == row + NR, 1.0, 0.0)
    scales = jnp.zeros((NR, KB), F32)
    block = 4
    for begin in range(0, NR, block):
        cols = [
            jnp.broadcast_to(aug[:, j : j + 1], (NR, KB)) for j in range(begin, begin + block)
        ]
        for m in range(block):
            j = begin + m
            pivot = cols[m][j : j + 1, :]
            root = jnp.where(pivot > floor, lax.rsqrt(jnp.maximum(pivot, 1e-30)), 0.0)
            factor = jnp.where(row > j, cols[m] * root, 0.0)
            aug = aug - factor * (aug[j : j + 1, :] * root)
            for later in range(m + 1, block):
                cols[later] = cols[later] - factor * (cols[later][j : j + 1, :] * root)
            scales = jnp.where(row == j, root, scales)
    return aug * scales


GROUP = 8


@functools.lru_cache(None)
def phase_tables():
    frequency = np.arange(KB) - KB // 2

    def make(period):
        angle = 2.0 * np.pi / period * np.mod(np.arange(period)[:, None] * frequency, period)
        return [
            turn(angle.astype(np.float32)).astype(ml_dtypes.bfloat16) for turn in (np.cos, np.sin)
        ]

    return make(TS) + make(TS + 2 * HALO)


@functools.lru_cache(None)
def imaging_tables(group):
    cosine, sine, column_cos, column_sin = [t.astype(np.float32) for t in phase_tables()]
    rows = TS // group
    turns, backs = [], []
    for rank in range(group):
        c, s = [t[rank * rows : (rank + 1) * rows] for t in (cosine, sine)]
        turns.append(np.block([[c, -s], [s, c]]))
        backs.append(np.block([[c.T, -s.T], [s.T, c.T]]))
    inner = slice(HALO, HALO + TS)
    inverse = np.concatenate([column_cos[inner], -column_sin[inner]], axis=1).T
    adjoint = np.concatenate([column_cos[inner], column_sin[inner]], axis=1)
    spread = np.concatenate([column_cos, -column_sin], axis=1).T
    return tuple(
        np.ascontiguousarray(t) for t in (np.stack(turns), np.stack(backs), inverse, adjoint, spread)
    )


def whole_kernel(
    slit_ref, zern_ref, points_ref, weight_ref, mask_ref, target_ref,
    basis_hbm, cos_hbm, sin_hbm, block_hbm, back_hbm, spread_hbm, turn_hbm, inverse_hbm, adjoint_hbm,
    out_ref,
    basis_ref, cos_ref, sin_ref, block_ref, back32_ref, spread32, turn32, inverse32, adjoint32,
    full, full_back, lag, lag_back,
    y_ref, z_ref, power_ref, pre_ref, pim_ref, edge_ref,
    held, wave_ref, field_ref, part_ref, got_ref, spart_ref, sgot_ref,
    acc_ref, rim_ref, left_ref, right_ref, mask_left, mask_right,
    local_sems, k_send, k_recv, g_send, g_recv, s_send, s_recv, r_send, r_recv, h_send, h_recv,
    *, group, line, tiles, rows, scale,
):
    rank, me = lax.axis_index("src"), lax.axis_index("tile")
    place = lax.rem(rank, tiles)
    right = lax.rem(me + 1, line)
    left = lax.rem(me + line - 1, line)
    peers = [lax.rem(rank + step, group) for step in range(1, group)]
    barrier = pltpu.get_barrier_semaphore()
    for peer in peers:
        pl.semaphore_signal(
            barrier, inc=1, device_id=(peer, me), device_id_type=pl.DeviceIdType.MESH
        )
    for side in (left, right):
        pl.semaphore_signal(
            barrier, inc=1, device_id=(rank, side), device_id_type=pl.DeviceIdType.MESH
        )
    loads = [
        (basis_hbm, basis_ref), (cos_hbm, cos_ref), (sin_hbm, sin_ref), (block_hbm, block_ref),
        (back_hbm.at[rank], back32_ref), (spread_hbm, spread32), (turn_hbm.at[rank], turn32),
        (inverse_hbm, inverse32), (adjoint_hbm, adjoint32),
    ]
    copies = [pltpu.make_async_copy(a, b, local_sems.at[i]) for i, (a, b) in enumerate(loads)]
    for copy in copies:
        copy.start()
    width = tiles * TS

    def send(src, dst, send_sem, recv_sem, device):
        copy = pltpu.make_async_remote_copy(
            src_ref=src, dst_ref=dst, send_sem=send_sem, recv_sem=recv_sem,
            device_id=device, device_id_type=pl.DeviceIdType.MESH,
        )
        copy.start()
        return copy

    halo_copies, spectrum_copies, kernel_copies = [], [], []

    def begin_exchange():
        pl.semaphore_wait(barrier, group - 1 + 2)
        ends = (mask_ref.at[:, width - 2 * HALO :], mask_ref.at[:, : 2 * HALO])
        halo_copies.append(send(ends[0], mask_left, h_send.at[0], h_recv.at[0], (rank, right)))
        halo_copies.append(send(ends[1], mask_right, h_send.at[1], h_recv.at[1], (rank, left)))

    def send_spectra():
        for copy in halo_copies:
            copy.wait_recv()
        for copy in copies[4:6]:
            copy.wait()
        spread = spread32[...].astype(BF16)
        back = back32_ref[...].astype(BF16)
        before = jnp.where(me > 0, mask_left[...].astype(F32), 0.0)
        after = jnp.where(me < line - 1, mask_right[...].astype(F32), 0.0)
        wide = lane_join([before, mask_ref[...].astype(F32), after])
        wide = pltpu.roll(wide, width + 3 * HALO, 1)
        for t in range(tiles):
            patch = wide[:, t * TS : (t + 1) * TS + 2 * HALO].astype(BF16)
            columns = lax.dot_general(
                patch, spread, (((1,), (1,)), ((), ())), preferred_element_type=F32
            ).astype(BF16)
            sums = dot(back, row_join([columns[:, :KB], -columns[:, KB:]]))
            spart_ref[t, 0] = sums[:KB].astype(BF16)
            spart_ref[t, 1] = (-sums[KB:]).astype(BF16)
        for step, peer in enumerate(peers):
            spectrum_copies.append(
                send(spart_ref, sgot_ref.at[step], s_send.at[step], s_recv.at[step], (peer, me))
            )

    lane = lax.broadcasted_iota(jnp.int32, (1, KB), 1)
    total = jnp.sum(weight_ref[...], axis=1, keepdims=True)
    weight = weight_ref[...] / (math.pi * RAD * RAD * total)
    px = SHIFT - points_ref[0:1, :]
    py = SHIFT - points_ref[1:2, :]
    count = points_ref.shape[1]
    hot_x = jnp.where(lax.broadcasted_iota(jnp.int32, (LP, count), 0) == px, weight, 0.0)
    lag_lane = lax.broadcasted_iota(jnp.int32, (KB, count), 0)
    hot_y = jnp.where(jnp.where(lag_lane < LP, lag_lane, lag_lane - LP) == py, 1.0, 0.0)
    omega = nt_mul(hot_x, hot_y)
    omega_cat = lane_join([omega[i : i + 1] for i in range(LAGS)])
    begin_exchange()
    copies[0].wait()
    slit = slit_ref[place]
    waves = zern_ref[slit, 0] * basis_ref[0]
    for z in range(1, NZ):
        waves = waves + zern_ref[slit, z] * basis_ref[z]
    inside = basis_ref[NZ]
    angle = 2.0 * math.pi * waves
    pr = inside * jnp.cos(angle)
    pi = inside * jnp.sin(angle)
    p40 = (pr[80:81, 40:41], pi[80:81, 40:41])
    m40 = (pr[0:1, 40:41], pi[0:1, 40:41])
    q40 = (pr[40:41, 80:81], pi[40:41, 80:81])
    n40 = (pr[40:41, 0:1], pi[40:41, 0:1])
    for copy in copies[1:3]:
        copy.wait()
    c, s = cos_ref[...], sin_ref[...]
    full32 = row_join([lane_join([c, -s]), lane_join([s, c])])
    back32 = row_join([lane_join([c, s]), lane_join([-s, c])])
    full[...] = full32.astype(BF16)
    full_back[...] = back32.astype(BF16)
    keep_row = lax.broadcasted_iota(jnp.int32, (LP, KB), 0) < LAGS
    cy, sy = jnp.where(keep_row, c[:LP], 0.0), jnp.where(keep_row, s[:LP], 0.0)
    lag[...] = row_join([lane_join([cy, -sy]), lane_join([sy, cy])]).astype(BF16)
    keep_lane = lax.broadcasted_iota(jnp.int32, (KB, KB), 1) < LAGS
    ct, st = jnp.where(keep_lane, c, 0.0), jnp.where(keep_lane, s, 0.0)
    lag_back[...] = row_join(
        [ct + pltpu.roll(st, LP, 1), pltpu.roll(ct, LP, 1) - st]
    ).astype(BF16)
    pupil = row_join([lane_join([pr, pi]), jnp.zeros((KB - DISC, 2 * KB), F32)])
    half = exact_dot(pupil, full32)
    hat = exact_dot(back32, row_join([half[:, :KB], half[:, KB:]]))
    hat = (hat[:KB], hat[KB:])
    unit = 1.0 / (KB * KB)
    pre_ref[...] = unit * hat[0]
    pim_ref[...] = unit * hat[1]
    power_ref[...] = unit * (hat[0] * hat[0] + hat[1] * hat[1])
    send_spectra()

    def times(scalar, re, im, conj):
        a, b = scalar
        b = -b if conj else b
        return a * re - b * im, a * im + b * re

    def entries(shape, items):
        row = lax.broadcasted_iota(jnp.int32, shape, 0)
        col = lax.broadcasted_iota(jnp.int32, shape, 1)
        matrix = jnp.zeros(shape, F32)
        for i, j, value in items:
            matrix = matrix + jnp.where((row == i) & (col == j), value, 0.0)
        return matrix.astype(BF16)

    end = LAGS - 1
    qr, qi = q40
    ar, ai = times(n40, qr, qi, True)
    start_fix = entries(
        (2 * KB, KB),
        [(0, end, -qr), (KB, end, -qi), (0, LP + end, qi), (KB, LP + end, -qr)],
    )
    gram_fix = entries(
        (KB, KB),
        [
            (end, 0, -ar), (LP + end, 0, ai), (LP + end, LP, -ar), (end, LP, -ai),
            (end, end, -1.0), (0, end, -ar), (LP, end, -ai),
            (LP + end, LP + end, -1.0), (LP, LP + end, -ar), (0, LP + end, ai),
        ],
    )
    final_fix = entries(
        (KB, 2 * KB),
        [(end, 0, -qr), (LP + end, 0, qi), (end, KB, -qi), (LP + end, KB, -qr)],
    )

    copies[3].wait()

    def lanes_of(x, g):
        return x[:, g * KB : (g + 1) * KB]

    def stack(x, rows):
        x = x.astype(BF16)
        pieces = [x[g * rows : (g + 1) * rows] for g in range(GROUP)]
        return row_join(
            [lane_join([p[:, :KB] for p in pieces]), lane_join([p[:, KB:] for p in pieces])]
        )

    def unstack(x):
        x = x.astype(BF16)
        rows = x.shape[0] // 2
        return row_join(
            [lane_join([lanes_of(x[:rows], g), lanes_of(x[rows:], g)]) for g in range(GROUP)]
        )

    def scaled(x, re, im):
        tops, lows = [], []
        for g in range(GROUP):
            hr, hi = lanes_of(x[:KB], g), lanes_of(x[KB:], g)
            if im is None:
                tops.append((re * hr).astype(BF16))
                lows.append((re * hi).astype(BF16))
            else:
                tops.append((re * hr - im * hi).astype(BF16))
                lows.append((re * hi + im * hr).astype(BF16))
        return row_join([lane_join(tops), lane_join(lows)])

    def start(group, carry):
        base = group * GROUP
        xs = [
            lane_join([block_ref[0, base + g].astype(BF16), block_ref[1, base + g].astype(BF16)])
            for g in range(GROUP)
        ]
        two = dot(full_back[...], stack(dot(row_join(xs), full[...]), KB))
        three = dot(lag[...], scaled(two, pre_ref[...], -pim_ref[...]))
        rims = row_join([x.astype(F32)[40 : 40 + LP].astype(BF16) for x in xs])
        c = dot(lane_join([unstack(three), rims]), row_join([lag_back[...], start_fix]))
        z_ref[pl.ds(pl.multiple_of(base * LP, GROUP * LP), GROUP * LP), :] = c
        return carry

    lax.fori_loop(0, NR // GROUP, start, 0)
    at_first = pl.ds(0, NR, stride=LP)
    at_last = pl.ds(end, NR, stride=LP)
    within = lane < LAGS
    er = row_join([block_ref[0, k, 0:1, :] for k in range(NR)])
    ei = row_join([block_ref[1, k, 0:1, :] for k in range(NR)])
    er = jnp.where(within, pltpu.roll(er, KB - 40, 1), 0.0)
    ei = jnp.where(within, pltpu.roll(ei, KB - 40, 1), 0.0)
    er, ei = times(p40, er, ei, True)
    z_ref[at_last, :] = z_ref[at_last, :] - (er + pltpu.roll(ei, LP, 1))

    def load_cat(ref):
        return lane_join([ref[pl.ds(i, NR, stride=LP), :] for i in range(LAGS)])

    def store_cat(ref, value):
        for i in range(LAGS):
            ref[pl.ds(i, NR, stride=LP), :] = value[:, i * KB : (i + 1) * KB]

    y_ref[...] = jnp.zeros_like(y_ref)
    store_cat(y_ref, load_cat(z_ref) * omega_cat)

    def turned(scalar_a, scalar_b, value):
        cr, ci = times(scalar_a, scalar_b[0], scalar_b[1], True)
        return cr * value + jnp.where(lane < LP, -ci, ci) * pltpu.roll(value, LP, 1)

    def apply_gram():
        def body(group, carry):
            base = pl.multiple_of(group * GROUP * LP, GROUP * LP)
            at = pl.ds(base, GROUP * LP)
            y = y_ref[at, :].astype(BF16)
            two = dot(lag_back[...], stack(dot(y, lag[...]), LP))
            three = dot(lag[...], scaled(two, power_ref[...], None))
            z_ref[at, :] = dot(
                lane_join([unstack(three), y]), row_join([lag_back[...], gram_fix])
            )
            return carry

        lax.fori_loop(0, NR // GROUP, body, 0, unroll=True)
        y_first, y_last = y_ref[at_first, :], y_ref[at_last, :]
        z_ref[at_first, :] = z_ref[at_first, :] - turned(m40, p40, y_last)
        z_ref[at_last, :] = z_ref[at_last, :] - (y_last + turned(p40, m40, y_first))

    eye = lax.broadcasted_iota(jnp.int32, (NR, NR), 0) == lax.broadcasted_iota(
        jnp.int32, (NR, NR), 1
    )

    def trace_of(m):
        return jnp.sum(
            jnp.sum(jnp.where(eye, m, 0.0), axis=1, keepdims=True), axis=0, keepdims=True
        )

    for it in range(ITERS):
        apply_gram()
        yc, zc = load_cat(y_ref), load_cat(z_ref)
        gram = nt_mul(yc, zc)
        ridge = RIDGE_SHARE * trace_of(gram) / NR + 1e-06
        gram = gram + jnp.where(eye, ridge, 0.0)
        inverse = eliminate(gram, 0.0)[:, NR : 2 * NR]
        projected = small_mul(inverse, zc)
        if it < ITERS - 1:
            store_cat(y_ref, projected * omega_cat)
        else:
            mixing = nt_mul(projected * omega_cat, projected)
            upper = eliminate(mixing, 1e-6 * trace_of(mixing))[:, :NR]
            store_cat(y_ref, small_mul(small_mul(upper, inverse), yc))

    last = y_ref[at_last, :]
    er = pltpu.roll(jnp.where(lane < LP, last, 0.0), 40, 1)
    ei = pltpu.roll(jnp.where(lane < LP, 0.0, last), 40 + LP, 1)
    er, ei = times(p40, er, ei, False)
    edge_ref[...] = lane_join([er, ei])

    for group_index in range(NR // GROUP):
        base = group_index * GROUP
        y = y_ref[base * LP : (base + GROUP) * LP, :].astype(BF16)
        two = dot(lag_back[...], stack(dot(y, lag[...]), LP))
        three = dot(full[...], scaled(two, pre_ref[...], pim_ref[...]))
        a = dot(unstack(three), full_back[...])
        fix = dot(y, final_fix)
        edges = edge_ref[base : base + GROUP, :]
        for g in range(GROUP):
            top = g * KB
            head = a[top : top + 8]
            first_row = lax.broadcasted_iota(jnp.int32, head.shape, 0) == 0
            head = head - jnp.where(first_row, edges[g : g + 1], 0.0)
            held[0, base + g] = row_join(
                [
                    head,
                    a[top + 8 : top + 40],
                    a[top + 40 : top + 40 + LP] + fix[g * LP : (g + 1) * LP],
                    a[top + 40 + LP : top + KB],
                ]
            ).astype(BF16)
        span = pl.ds(base, GROUP)
        for step in range(1, tiles):
            kernel_copies.append(
                send(
                    held.at[0, span], held.at[step, span], k_send.at[step - 1, group_index],
                    k_recv.at[step - 1, group_index],
                    (rank - place + lax.rem(place + step, tiles), me),
                )
            )

    copies[6].wait()
    turn = turn32[...].astype(BF16)
    back = back32_ref[...].astype(BF16)
    spread = spread32[...].astype(BF16)
    for load in copies[7:]:
        load.wait()
    inverse = inverse32[...].astype(BF16)
    adjoint = adjoint32[...].astype(BF16)

    def parts(block):
        return block[:, :KB].astype(F32), block[:, KB:].astype(F32)

    for copy in spectrum_copies:
        copy.wait_recv()
    grad_copies = []
    for slot in range(tiles):
        t = lax.rem(place + tiles - slot, tiles)
        start = pl.multiple_of(t * TS, TS)
        if slot > 0:
            for copy in kernel_copies[slot - 1 :: tiles - 1]:
                copy.wait_recv()
        spectrum = spart_ref[t].astype(F32)
        for step in range(group - 1):
            spectrum = spectrum + sgot_ref[step, t].astype(F32)
        sre, sim = scale * spectrum[0], scale * spectrum[1]

        def forward(pair, carry):
            w = []
            for q in range(2):
                kr, ki = parts(held[slot, 2 * pair + q])
                w.append(((kr * sre + ki * sim).astype(BF16), (kr * sim - ki * sre).astype(BF16)))
            both = row_join([lane_join([w[0][h], w[1][h]]) for h in range(2)])
            turned = dot(turn, both).astype(BF16)
            for q in range(2):
                at = pl.ds(pl.multiple_of((2 * pair + q) * rows, rows), rows)
                lanes = slice(q * KB, (q + 1) * KB)
                wave_ref[at, :] = lane_join([turned[:rows, lanes], turned[rows:, lanes]])
            return carry

        lax.fori_loop(0, NR // 2, forward, 0, unroll=4)
        field_ref[...] = dot(wave_ref[...], inverse)

        def energy(k, total):
            field = field_ref[pl.ds(pl.multiple_of(k * rows, rows), rows), :]
            return total + field * field

        intensity = lax.fori_loop(0, NR, energy, jnp.zeros((rows, TS), F32), unroll=4)
        resist = 1.0 / (1.0 + jnp.exp(-STEEPNESS * (intensity - THRESHOLD)))
        goal = target_ref[:, pl.ds(start, TS)].astype(F32)
        out_ref[0, :, pl.ds(start, TS)] = resist.astype(BF16)
        slope = 4.0 * (resist - goal) * STEEPNESS * resist * (1.0 - resist)

        def weigh(k, carry):
            at = pl.ds(pl.multiple_of(k * rows, rows), rows)
            wave_ref[at, :] = (field_ref[at, :] * slope).astype(BF16)
            return carry

        lax.fori_loop(0, NR, weigh, 0, unroll=4)
        wave_ref[...] = dot(wave_ref[...], adjoint).astype(BF16)

        def gather(pair, carry):
            acc_re, acc_im = carry
            waves = [
                wave_ref[pl.ds(pl.multiple_of((2 * pair + q) * rows, rows), rows), :]
                for q in range(2)
            ]
            both = row_join(
                [lane_join([waves[q][:, h * KB : (h + 1) * KB] for q in range(2)]) for h in range(2)]
            )
            turned = dot(back, both)
            for q in range(2):
                kr, ki = parts(held[slot, 2 * pair + q])
                tr = turned[:KB, q * KB : (q + 1) * KB]
                ti = turned[KB:, q * KB : (q + 1) * KB]
                acc_re = acc_re + kr * tr + ki * ti
                acc_im = acc_im + ki * tr - kr * ti
            return acc_re, acc_im

        zero = jnp.zeros((KB, KB), F32)
        acc_re, acc_im = lax.fori_loop(0, NR // 2, gather, (zero, zero), unroll=4)
        part_ref[slot, 0] = acc_re.astype(BF16)
        part_ref[slot, 1] = acc_im.astype(BF16)
        grad_copies.append(
            [
                send(
                    part_ref.at[slot], got_ref.at[slot, step], g_send.at[slot, step],
                    g_recv.at[slot, step], (peer, me),
                )
                for step, peer in enumerate(peers)
            ]
        )

    acc_ref[...] = jnp.zeros_like(acc_ref)
    for copies in grad_copies:
        for copy in copies:
            copy.wait_recv()
    for slot in range(tiles):
        t = lax.rem(place + tiles - slot, tiles)
        at = pl.ds(pl.multiple_of(t * TS, TS), TS + 2 * HALO)
        total = part_ref[slot].astype(F32)
        for step in range(1, group):
            total = total + got_ref[(slot - step) % tiles, step - 1].astype(F32)
        total = (scale * total).astype(BF16)
        rows_back = dot(turn, row_join([total[0], total[1]])).astype(BF16)
        patch = dot(lane_join([rows_back[:rows], rows_back[rows:]]), spread)
        acc_ref[:, at] = acc_ref[:, at] + patch

    lane = lax.broadcasted_iota(jnp.int32, (rows, 2 * HALO), 1)
    low = lane < HALO
    rim_ref[...] = jnp.where(
        low, acc_ref[:, : 2 * HALO], acc_ref[:, width : width + 2 * HALO]
    ).astype(BF16)
    rims = [
        send(rim_ref, left_ref, r_send.at[0], r_recv.at[0], (rank, right)),
        send(rim_ref, right_ref, r_send.at[1], r_recv.at[1], (rank, left)),
    ]
    inner = pltpu.roll(acc_ref[...], width + HALO, 1)[:, :width]
    rims[0].wait_recv()
    rims[1].wait_recv()
    from_left = pltpu.roll(left_ref[...].astype(F32), HALO, 1)
    from_right = pltpu.roll(right_ref[...].astype(F32), HALO, 1)
    from_left = jnp.where(low & (me > 0), from_left, 0.0)
    from_right = jnp.where((lane >= HALO) & (me < line - 1), from_right, 0.0)
    blocks = [
        inner[:, : 2 * HALO] + from_left,
        inner[:, 2 * HALO : width - 2 * HALO],
        inner[:, width - 2 * HALO :] + from_right,
    ]
    out_ref[1] = lane_join(blocks).astype(BF16)
    for copy in halo_copies + spectrum_copies + kernel_copies + [c for copies in grad_copies for c in copies] + rims:
        copy.wait_send()


def on_device(mask, target, start_block, zernike, source_points, source_weight, tile_slit):
    tiles = tile_slit.shape[0]
    rows = mask.shape[0]
    group, line = lax.axis_size("src"), lax.axis_size("tile")
    scale = 1.0 / math.sqrt(TS * (TS + 2 * HALO))
    turns, backs, inverse, adjoint, spread = imaging_tables(group)
    cosine, sine = dft_tables()
    held = [
        jnp.asarray(t)
        for t in (zernike_table(), cosine, sine, start_block, backs, spread, turns, inverse, adjoint)
    ]
    vmem = pl.BlockSpec(memory_space=pltpu.VMEM)
    smem = pl.BlockSpec(memory_space=pltpu.SMEM)
    hbm = pl.BlockSpec(memory_space=pl.ANY)
    dma = pltpu.SemaphoreType.DMA
    own = [x.shape[1:] if x.shape[0] == group and x.ndim == 3 else x.shape for x in held]
    steps = group - 1
    scratch = [pltpu.VMEM(shape, F32) for shape in own]
    scratch += [
        pltpu.VMEM(shape, BF16)
        for shape in [(2 * KB, 2 * KB), (2 * KB, 2 * KB), (KB, 2 * KB), (2 * KB, KB)]
    ]
    scratch += [
        pltpu.VMEM(shape, F32)
        for shape in [(NR * LP, KB), (NR * LP, KB), (KB, KB), (KB, KB), (KB, KB), (NR, 2 * KB)]
    ]
    scratch += [
        pltpu.VMEM((tiles, NR, KB, 2 * KB), BF16),
        pltpu.VMEM((NR * rows, TS), BF16),
        pltpu.VMEM((NR * rows, TS), F32),
        pltpu.VMEM((tiles, 2, KB, KB), BF16),
        pltpu.VMEM((tiles, steps, 2, KB, KB), BF16),
        pltpu.VMEM((tiles, 2, KB, KB), BF16),
        pltpu.VMEM((steps, tiles, 2, KB, KB), BF16),
        pltpu.VMEM((rows, tiles * TS + 2 * HALO), F32),
    ]
    scratch += [pltpu.VMEM((rows, 2 * HALO), BF16)] * 5
    scratch += [
        dma((len(held),)), dma((tiles, NR // GROUP)), dma((tiles, NR // GROUP)),
        dma((tiles, steps)), dma((tiles, steps)), dma((steps,)), dma((steps,)),
        dma((2,)), dma((2,)), dma((2,)), dma((2,)),
    ]
    out = pl.pallas_call(
        functools.partial(
            whole_kernel, group=group, line=line, tiles=tiles, rows=rows, scale=scale
        ),
        out_shape=jax.ShapeDtypeStruct((2,) + target.shape, BF16),
        in_specs=[smem, smem] + [vmem] * 4 + [hbm] * len(held),
        out_specs=vmem,
        scratch_shapes=scratch,
        compiler_params=pltpu.CompilerParams(
            vmem_limit_bytes=56 * 2**20, collective_id=0, has_side_effects=True
        ),
        cost_estimate=pl.CostEstimate(
            flops=8 * 10**9, bytes_accessed=8 * 10**6, transcendentals=0
        ),
    )(tile_slit, zernike, source_points.T, source_weight[None, :], mask, target, *held)
    return out[0], out[1]


def solution(mesh):
    placed = (P("src", "tile"), P("src", "tile"), P(), P(), P(), P(), P("tile"))
    return jax.shard_map(
        on_device,
        mesh=mesh,
        in_specs=placed,
        out_specs=(P("src", "tile"), P("src", "tile")),
        check_vma=False,
    )
```

```python
import functools
import math

import jax
import jax.numpy as jnp
import ml_dtypes
import numpy as np
from jax import lax
from jax.experimental import pallas as pl
from jax.experimental.pallas import tpu as pltpu
from jax.sharding import PartitionSpec as P

KB = 128
NR = 24
NZ = 37
RAD = 40
SHIFT = 24
HALO = 64
ITERS = 4
TS = 256
LAGS = 2 * SHIFT + 1
LP = 64
DISC = 88

STEEPNESS = 4.0
THRESHOLD = 0.5
RIDGE_SHARE = 0.001
F32 = jnp.float32
BF16 = jnp.bfloat16


def noll_terms(term_count):
    listing = []
    degree = 0
    while len(listing) < term_count:
        for azimuth in range(degree % 2, degree + 1, 2):
            if azimuth == 0:
                listing.append((degree, 0, 0))
            else:
                for repeat in range(2):
                    number = len(listing) + 1
                    listing.append((degree, azimuth, 2 if number % 2 == 0 else 1))
        degree += 1
    return listing[:term_count]


def radial_terms(degree, azimuth):
    powers = []
    for counter in range((degree - azimuth) // 2 + 1):
        factor = (
            (-1) ** counter
            * math.factorial(degree - counter)
            / (
                math.factorial(counter)
                * math.factorial((degree + azimuth) // 2 - counter)
                * math.factorial((degree - azimuth) // 2 - counter)
            )
        )
        powers.append((degree - 2 * counter, factor))
    return powers


@functools.lru_cache(None)
def zernike_table():
    u = (np.arange(DISC) - RAD)[:, None]
    v = (np.arange(KB) - RAD)[None, :]
    inside = (u * u + v * v <= RAD * RAD).astype(np.float64)
    rho = np.sqrt(u * u + v * v) / RAD
    theta = np.arctan2(v + 0.0 * u, u + 0.0 * v)
    planes = []
    for degree, azimuth, parity in noll_terms(NZ):
        radial = sum(f * rho**e for e, f in radial_terms(degree, azimuth))
        if azimuth == 0:
            plane = math.sqrt(degree + 1.0) * radial
        else:
            turn = np.cos if parity == 2 else np.sin
            plane = math.sqrt(2.0 * degree + 2.0) * radial * turn(azimuth * theta)
        planes.append(plane * inside)
    planes.append(inside)
    return np.stack(planes).astype(np.float32)


@functools.lru_cache(None)
def dft_tables():
    f = np.arange(KB)
    angle = 2.0 * np.pi / KB * ((f[:, None] * f[None, :]) % KB)
    return np.cos(angle).astype(np.float32), np.sin(angle).astype(np.float32)


def halves(x):
    high = x.astype(BF16)
    return high, (x - high.astype(F32)).astype(BF16)


def dot(x, y):
    return jnp.dot(x.astype(BF16), y.astype(BF16), preferred_element_type=F32)


def split(x):
    high = x.astype(BF16).astype(F32)
    return high, x - high


def nt_mul(x, y):
    n, m = x.shape[0], y.shape[0]
    left = jnp.concatenate(split(x), axis=0).astype(BF16)
    right = jnp.concatenate(split(y), axis=0).astype(BF16)
    out = lax.dot_general(left, right, (((1,), (1,)), ((), ())), preferred_element_type=F32)
    return out[:n, :m] + out[n:, :m] + out[:n, m:]


def small_mul(m, x):
    mh, ml = split(m)
    xh, xl = split(x)
    return dot(lane_join([mh, mh, ml]), row_join([xh, xl, xh]))


def exact_dot(x, y):
    xh, xl = halves(x)
    yh, yl = halves(y)
    return dot(xh, yh) + dot(xl, yh) + dot(xh, yl)


def lane_join(parts):
    return jnp.concatenate(parts, axis=1)


def row_join(parts):
    return jnp.concatenate(parts, axis=0)


def eliminate(gram, floor):
    row = lax.broadcasted_iota(jnp.int32, (NR, KB), 0)
    lane = lax.broadcasted_iota(jnp.int32, (NR, KB), 1)
    aug = lane_join([gram, jnp.zeros((NR, KB - NR), F32)])
    aug = aug + jnp.where(lane == row + NR, 1.0, 0.0)
    scales = jnp.zeros((NR, KB), F32)
    block = 8
    for begin in range(0, NR, block):
        cols = [
            jnp.broadcast_to(aug[:, j : j + 1], (NR, KB)) for j in range(begin, begin + block)
        ]
        for m in range(block):
            j = begin + m
            pivot = cols[m][j : j + 1, :]
            root = jnp.where(pivot > floor, lax.rsqrt(jnp.maximum(pivot, 1e-30)), 0.0)
            factor = jnp.where(row > j, cols[m] * root, 0.0)
            aug = aug - factor * (aug[j : j + 1, :] * root)
            for later in range(m + 1, block):
                cols[later] = cols[later] - factor * (cols[later][j : j + 1, :] * root)
            scales = jnp.where(row == j, root, scales)
    return aug * scales


GROUP = 8


@functools.lru_cache(None)
def phase_tables():
    frequency = np.arange(KB) - KB // 2

    def make(period):
        angle = 2.0 * np.pi / period * np.mod(np.arange(period)[:, None] * frequency, period)
        return [
            turn(angle.astype(np.float32)).astype(ml_dtypes.bfloat16) for turn in (np.cos, np.sin)
        ]

    return make(TS) + make(TS + 2 * HALO)


@functools.lru_cache(None)
def imaging_tables(group):
    cosine, sine, column_cos, column_sin = [t.astype(np.float32) for t in phase_tables()]
    rows = TS // group
    turns, backs = [], []
    for rank in range(group):
        c, s = [t[rank * rows : (rank + 1) * rows] for t in (cosine, sine)]
        turns.append(np.block([[c, -s], [s, c]]))
        backs.append(np.block([[c.T, -s.T], [s.T, c.T]]))
    inner = slice(HALO, HALO + TS)
    inverse = np.concatenate([column_cos[inner], -column_sin[inner]], axis=1).T
    adjoint = np.concatenate([column_cos[inner], column_sin[inner]], axis=1)
    spread = np.concatenate([column_cos, -column_sin], axis=1).T
    return tuple(
        np.ascontiguousarray(t) for t in (np.stack(turns), np.stack(backs), inverse, adjoint, spread)
    )


def whole_kernel(
    slit_ref, zern_ref, points_ref, weight_ref, mask_ref, target_ref,
    basis_hbm, cos_hbm, sin_hbm, block_hbm, back_hbm, spread_hbm, turn_hbm, inverse_hbm, adjoint_hbm,
    out_ref,
    basis_ref, cos_ref, sin_ref, block_ref, back32_ref, spread32, turn32, inverse32, adjoint32,
    full, full_back, lag, lag_back,
    y_ref, z_ref, power_ref, pre_ref, pim_ref, edge_ref,
    held, wave_ref, field_ref, part_ref, got_ref, spart_ref, sgot_ref,
    acc_ref, rim_ref, left_ref, right_ref, mask_left, mask_right,
    local_sems, k_send, k_recv, g_send, g_recv, s_send, s_recv, r_send, r_recv, h_send, h_recv,
    *, group, line, tiles, rows, scale,
):
    rank, me = lax.axis_index("src"), lax.axis_index("tile")
    place = lax.rem(rank, tiles)
    right = lax.rem(me + 1, line)
    left = lax.rem(me + line - 1, line)
    peers = [lax.rem(rank + step, group) for step in range(1, group)]
    barrier = pltpu.get_barrier_semaphore()
    for peer in peers:
        pl.semaphore_signal(
            barrier, inc=1, device_id=(peer, me), device_id_type=pl.DeviceIdType.MESH
        )
    for side in (left, right):
        pl.semaphore_signal(
            barrier, inc=1, device_id=(rank, side), device_id_type=pl.DeviceIdType.MESH
        )
    loads = [
        (basis_hbm, basis_ref), (cos_hbm, cos_ref), (sin_hbm, sin_ref), (block_hbm, block_ref),
        (back_hbm.at[rank], back32_ref), (spread_hbm, spread32), (turn_hbm.at[rank], turn32),
        (inverse_hbm, inverse32), (adjoint_hbm, adjoint32),
    ]
    copies = [pltpu.make_async_copy(a, b, local_sems.at[i]) for i, (a, b) in enumerate(loads)]
    for copy in copies:
        copy.start()
    width = tiles * TS

    def send(src, dst, send_sem, recv_sem, device):
        copy = pltpu.make_async_remote_copy(
            src_ref=src, dst_ref=dst, send_sem=send_sem, recv_sem=recv_sem,
            device_id=device, device_id_type=pl.DeviceIdType.MESH,
        )
        copy.start()
        return copy

    halo_copies, spectrum_copies, kernel_copies = [], [], []

    def begin_exchange():
        pl.semaphore_wait(barrier, group - 1 + 2)
        ends = (mask_ref.at[:, width - 2 * HALO :], mask_ref.at[:, : 2 * HALO])
        halo_copies.append(send(ends[0], mask_left, h_send.at[0], h_recv.at[0], (rank, right)))
        halo_copies.append(send(ends[1], mask_right, h_send.at[1], h_recv.at[1], (rank, left)))

    def send_spectra():
        for copy in halo_copies:
            copy.wait_recv()
        for copy in copies[4:6]:
            copy.wait()
        spread = spread32[...].astype(BF16)
        back = back32_ref[...].astype(BF16)
        before = jnp.where(me > 0, mask_left[...].astype(F32), 0.0)
        after = jnp.where(me < line - 1, mask_right[...].astype(F32), 0.0)
        wide = lane_join([before, mask_ref[...].astype(F32), after])
        wide = pltpu.roll(wide, width + 3 * HALO, 1)
        for t in range(tiles):
            patch = wide[:, t * TS : (t + 1) * TS + 2 * HALO].astype(BF16)
            columns = lax.dot_general(
                patch, spread, (((1,), (1,)), ((), ())), preferred_element_type=F32
            ).astype(BF16)
            sums = dot(back, row_join([columns[:, :KB], -columns[:, KB:]]))
            spart_ref[t, 0] = sums[:KB].astype(BF16)
            spart_ref[t, 1] = (-sums[KB:]).astype(BF16)
        for step, peer in enumerate(peers):
            spectrum_copies.append(
                send(spart_ref, sgot_ref.at[step], s_send.at[step], s_recv.at[step], (peer, me))
            )

    lane = lax.broadcasted_iota(jnp.int32, (1, KB), 1)
    total = jnp.sum(weight_ref[...], axis=1, keepdims=True)
    weight = weight_ref[...] / (math.pi * RAD * RAD * total)
    px = SHIFT - points_ref[0:1, :]
    py = SHIFT - points_ref[1:2, :]
    count = points_ref.shape[1]
    hot_x = jnp.where(lax.broadcasted_iota(jnp.int32, (LP, count), 0) == px, weight, 0.0)
    lag_lane = lax.broadcasted_iota(jnp.int32, (KB, count), 0)
    hot_y = jnp.where(jnp.where(lag_lane < LP, lag_lane, lag_lane - LP) == py, 1.0, 0.0)
    omega = nt_mul(hot_x, hot_y)
    omega_cat = lane_join([omega[i : i + 1] for i in range(LAGS)])
    begin_exchange()
    copies[0].wait()
    slit = slit_ref[place]
    waves = zern_ref[slit, 0] * basis_ref[0]
    for z in range(1, NZ):
        waves = waves + zern_ref[slit, z] * basis_ref[z]
    inside = basis_ref[NZ]
    angle = 2.0 * math.pi * waves
    pr = inside * jnp.cos(angle)
    pi = inside * jnp.sin(angle)
    p40 = (pr[80:81, 40:41], pi[80:81, 40:41])
    m40 = (pr[0:1, 40:41], pi[0:1, 40:41])
    q40 = (pr[40:41, 80:81], pi[40:41, 80:81])
    n40 = (pr[40:41, 0:1], pi[40:41, 0:1])
    for copy in copies[1:3]:
        copy.wait()
    c, s = cos_ref[...], sin_ref[...]
    full32 = row_join([lane_join([c, -s]), lane_join([s, c])])
    back32 = row_join([lane_join([c, s]), lane_join([-s, c])])
    full[...] = full32.astype(BF16)
    full_back[...] = back32.astype(BF16)
    keep_row = lax.broadcasted_iota(jnp.int32, (LP, KB), 0) < LAGS
    cy, sy = jnp.where(keep_row, c[:LP], 0.0), jnp.where(keep_row, s[:LP], 0.0)
    lag[...] = row_join([lane_join([cy, -sy]), lane_join([sy, cy])]).astype(BF16)
    keep_lane = lax.broadcasted_iota(jnp.int32, (KB, KB), 1) < LAGS
    ct, st = jnp.where(keep_lane, c, 0.0), jnp.where(keep_lane, s, 0.0)
    lag_back[...] = row_join(
        [ct + pltpu.roll(st, LP, 1), pltpu.roll(ct, LP, 1) - st]
    ).astype(BF16)
    pupil = row_join([lane_join([pr, pi]), jnp.zeros((KB - DISC, 2 * KB), F32)])
    half = exact_dot(pupil, full32)
    hat = exact_dot(back32, row_join([half[:, :KB], half[:, KB:]]))
    hat = (hat[:KB], hat[KB:])
    unit = 1.0 / (KB * KB)
    pre_ref[...] = unit * hat[0]
    pim_ref[...] = unit * hat[1]
    power_ref[...] = unit * (hat[0] * hat[0] + hat[1] * hat[1])
    send_spectra()

    def times(scalar, re, im, conj):
        a, b = scalar
        b = -b if conj else b
        return a * re - b * im, a * im + b * re

    def entries(shape, items):
        row = lax.broadcasted_iota(jnp.int32, shape, 0)
        col = lax.broadcasted_iota(jnp.int32, shape, 1)
        matrix = jnp.zeros(shape, F32)
        for i, j, value in items:
            matrix = matrix + jnp.where((row == i) & (col == j), value, 0.0)
        return matrix.astype(BF16)

    end = LAGS - 1
    qr, qi = q40
    ar, ai = times(n40, qr, qi, True)
    start_fix = entries(
        (2 * KB, KB),
        [(0, end, -qr), (KB, end, -qi), (0, LP + end, qi), (KB, LP + end, -qr)],
    )
    gram_fix = entries(
        (KB, KB),
        [
            (end, 0, -ar), (LP + end, 0, ai), (LP + end, LP, -ar), (end, LP, -ai),
            (end, end, -1.0), (0, end, -ar), (LP, end, -ai),
            (LP + end, LP + end, -1.0), (LP, LP + end, -ar), (0, LP + end, ai),
        ],
    )
    final_fix = entries(
        (KB, 2 * KB),
        [(end, 0, -qr), (LP + end, 0, qi), (end, KB, -qi), (LP + end, KB, -qr)],
    )

    copies[3].wait()

    def lanes_of(x, g):
        return x[:, g * KB : (g + 1) * KB]

    def stack(x, rows):
        x = x.astype(BF16)
        pieces = [x[g * rows : (g + 1) * rows] for g in range(GROUP)]
        return row_join(
            [lane_join([p[:, :KB] for p in pieces]), lane_join([p[:, KB:] for p in pieces])]
        )

    def unstack(x):
        x = x.astype(BF16)
        rows = x.shape[0] // 2
        return row_join(
            [lane_join([lanes_of(x[:rows], g), lanes_of(x[rows:], g)]) for g in range(GROUP)]
        )

    def scaled(x, re, im):
        tops, lows = [], []
        for g in range(GROUP):
            hr, hi = lanes_of(x[:KB], g), lanes_of(x[KB:], g)
            if im is None:
                tops.append((re * hr).astype(BF16))
                lows.append((re * hi).astype(BF16))
            else:
                tops.append((re * hr - im * hi).astype(BF16))
                lows.append((re * hi + im * hr).astype(BF16))
        return row_join([lane_join(tops), lane_join(lows)])

    def start(group, carry):
        base = group * GROUP
        xs = [
            lane_join([block_ref[0, base + g].astype(BF16), block_ref[1, base + g].astype(BF16)])
            for g in range(GROUP)
        ]
        two = dot(full_back[...], stack(dot(row_join(xs), full[...]), KB))
        three = dot(lag[...], scaled(two, pre_ref[...], -pim_ref[...]))
        rims = row_join([x.astype(F32)[40 : 40 + LP].astype(BF16) for x in xs])
        c = dot(lane_join([unstack(three), rims]), row_join([lag_back[...], start_fix]))
        z_ref[pl.ds(pl.multiple_of(base * LP, GROUP * LP), GROUP * LP), :] = c
        return carry

    lax.fori_loop(0, NR // GROUP, start, 0, unroll=True)
    at_first = pl.ds(0, NR, stride=LP)
    at_last = pl.ds(end, NR, stride=LP)
    within = lane < LAGS
    er = row_join([block_ref[0, k, 0:1, :] for k in range(NR)])
    ei = row_join([block_ref[1, k, 0:1, :] for k in range(NR)])
    er = jnp.where(within, pltpu.roll(er, KB - 40, 1), 0.0)
    ei = jnp.where(within, pltpu.roll(ei, KB - 40, 1), 0.0)
    er, ei = times(p40, er, ei, True)
    z_ref[at_last, :] = z_ref[at_last, :] - (er + pltpu.roll(ei, LP, 1))

    def load_cat(ref):
        return lane_join([ref[pl.ds(i, NR, stride=LP), :] for i in range(LAGS)])

    def store_cat(ref, value):
        for i in range(LAGS):
            ref[pl.ds(i, NR, stride=LP), :] = value[:, i * KB : (i + 1) * KB]

    y_ref[...] = jnp.zeros_like(y_ref)
    store_cat(y_ref, load_cat(z_ref) * omega_cat)

    def turned(scalar_a, scalar_b, value):
        cr, ci = times(scalar_a, scalar_b[0], scalar_b[1], True)
        return cr * value + jnp.where(lane < LP, -ci, ci) * pltpu.roll(value, LP, 1)

    def apply_gram():
        def body(group, carry):
            base = pl.multiple_of(group * GROUP * LP, GROUP * LP)
            at = pl.ds(base, GROUP * LP)
            y = y_ref[at, :].astype(BF16)
            two = dot(lag_back[...], stack(dot(y, lag[...]), LP))
            three = dot(lag[...], scaled(two, power_ref[...], None))
            z_ref[at, :] = dot(
                lane_join([unstack(three), y]), row_join([lag_back[...], gram_fix])
            )
            return carry

        lax.fori_loop(0, NR // GROUP, body, 0, unroll=True)
        y_first, y_last = y_ref[at_first, :], y_ref[at_last, :]
        z_ref[at_first, :] = z_ref[at_first, :] - turned(m40, p40, y_last)
        z_ref[at_last, :] = z_ref[at_last, :] - (y_last + turned(p40, m40, y_first))

    eye = lax.broadcasted_iota(jnp.int32, (NR, NR), 0) == lax.broadcasted_iota(
        jnp.int32, (NR, NR), 1
    )

    def trace_of(m):
        return jnp.sum(
            jnp.sum(jnp.where(eye, m, 0.0), axis=1, keepdims=True), axis=0, keepdims=True
        )

    for it in range(ITERS):
        apply_gram()
        yc, zc = load_cat(y_ref), load_cat(z_ref)
        gram = nt_mul(yc, zc)
        ridge = RIDGE_SHARE * trace_of(gram) / NR + 1e-06
        gram = gram + jnp.where(eye, ridge, 0.0)
        inverse = eliminate(gram, 0.0)[:, NR : 2 * NR]
        projected = small_mul(inverse, zc)
        if it < ITERS - 1:
            store_cat(y_ref, projected * omega_cat)
        else:
            mixing = nt_mul(projected * omega_cat, projected)
            upper = eliminate(mixing, 1e-6 * trace_of(mixing))[:, :NR]
            store_cat(y_ref, small_mul(small_mul(upper, inverse), yc))

    last = y_ref[at_last, :]
    er = pltpu.roll(jnp.where(lane < LP, last, 0.0), 40, 1)
    ei = pltpu.roll(jnp.where(lane < LP, 0.0, last), 40 + LP, 1)
    er, ei = times(p40, er, ei, False)
    edge_ref[...] = lane_join([er, ei])

    for group_index in range(NR // GROUP):
        base = group_index * GROUP
        y = y_ref[base * LP : (base + GROUP) * LP, :].astype(BF16)
        two = dot(lag_back[...], stack(dot(y, lag[...]), LP))
        three = dot(full[...], scaled(two, pre_ref[...], pim_ref[...]))
        a = dot(unstack(three), full_back[...])
        fix = dot(y, final_fix)
        edges = edge_ref[base : base + GROUP, :]
        for g in range(GROUP):
            top = g * KB
            head = a[top : top + 8]
            first_row = lax.broadcasted_iota(jnp.int32, head.shape, 0) == 0
            head = head - jnp.where(first_row, edges[g : g + 1], 0.0)
            held[0, base + g] = row_join(
                [
                    head,
                    a[top + 8 : top + 40],
                    a[top + 40 : top + 40 + LP] + fix[g * LP : (g + 1) * LP],
                    a[top + 40 + LP : top + KB],
                ]
            ).astype(BF16)
        span = pl.ds(base, GROUP)
        for step in range(1, tiles):
            kernel_copies.append(
                send(
                    held.at[0, span], held.at[step, span], k_send.at[step - 1, group_index],
                    k_recv.at[step - 1, group_index],
                    (rank - place + lax.rem(place + step, tiles), me),
                )
            )

    copies[6].wait()
    turn = turn32[...].astype(BF16)
    back = back32_ref[...].astype(BF16)
    spread = spread32[...].astype(BF16)
    for load in copies[7:]:
        load.wait()
    inverse = inverse32[...].astype(BF16)
    adjoint = adjoint32[...].astype(BF16)

    def parts(block):
        return block[:, :KB].astype(F32), block[:, KB:].astype(F32)

    for copy in spectrum_copies:
        copy.wait_recv()
    grad_copies = []
    for slot in range(tiles):
        t = lax.rem(place + tiles - slot, tiles)
        start = pl.multiple_of(t * TS, TS)
        if slot > 0:
            for copy in kernel_copies[slot - 1 :: tiles - 1]:
                copy.wait_recv()
        spectrum = spart_ref[t].astype(F32)
        for step in range(group - 1):
            spectrum = spectrum + sgot_ref[step, t].astype(F32)
        sre, sim = scale * spectrum[0], scale * spectrum[1]

        def forward(pair, carry):
            w = []
            for q in range(2):
                kr, ki = parts(held[slot, 2 * pair + q])
                w.append(((kr * sre + ki * sim).astype(BF16), (kr * sim - ki * sre).astype(BF16)))
            both = row_join([lane_join([w[0][h], w[1][h]]) for h in range(2)])
            turned = dot(turn, both).astype(BF16)
            for q in range(2):
                at = pl.ds(pl.multiple_of((2 * pair + q) * rows, rows), rows)
                lanes = slice(q * KB, (q + 1) * KB)
                wave_ref[at, :] = lane_join([turned[:rows, lanes], turned[rows:, lanes]])
            return carry

        lax.fori_loop(0, NR // 2, forward, 0, unroll=4)
        field_ref[...] = dot(wave_ref[...], inverse)

        def energy(k, total):
            field = field_ref[pl.ds(pl.multiple_of(k * rows, rows), rows), :]
            return total + field * field

        intensity = lax.fori_loop(0, NR, energy, jnp.zeros((rows, TS), F32), unroll=4)
        resist = 1.0 / (1.0 + jnp.exp(-STEEPNESS * (intensity - THRESHOLD)))
        goal = target_ref[:, pl.ds(start, TS)].astype(F32)
        out_ref[0, :, pl.ds(start, TS)] = resist.astype(BF16)
        slope = 4.0 * (resist - goal) * STEEPNESS * resist * (1.0 - resist)

        def weigh(k, carry):
            at = pl.ds(pl.multiple_of(k * rows, rows), rows)
            wave_ref[at, :] = (field_ref[at, :] * slope).astype(BF16)
            return carry

        lax.fori_loop(0, NR, weigh, 0, unroll=4)
        wave_ref[...] = dot(wave_ref[...], adjoint).astype(BF16)

        def gather(pair, carry):
            acc_re, acc_im = carry
            waves = [
                wave_ref[pl.ds(pl.multiple_of((2 * pair + q) * rows, rows), rows), :]
                for q in range(2)
            ]
            both = row_join(
                [lane_join([waves[q][:, h * KB : (h + 1) * KB] for q in range(2)]) for h in range(2)]
            )
            turned = dot(back, both)
            for q in range(2):
                kr, ki = parts(held[slot, 2 * pair + q])
                tr = turned[:KB, q * KB : (q + 1) * KB]
                ti = turned[KB:, q * KB : (q + 1) * KB]
                acc_re = acc_re + kr * tr + ki * ti
                acc_im = acc_im + ki * tr - kr * ti
            return acc_re, acc_im

        zero = jnp.zeros((KB, KB), F32)
        acc_re, acc_im = lax.fori_loop(0, NR // 2, gather, (zero, zero), unroll=4)
        part_ref[slot, 0] = acc_re.astype(BF16)
        part_ref[slot, 1] = acc_im.astype(BF16)
        grad_copies.append(
            [
                send(
                    part_ref.at[slot], got_ref.at[slot, step], g_send.at[slot, step],
                    g_recv.at[slot, step], (peer, me),
                )
                for step, peer in enumerate(peers)
            ]
        )

    acc_ref[...] = jnp.zeros_like(acc_ref)
    for copies in grad_copies:
        for copy in copies:
            copy.wait_recv()
    for slot in range(tiles):
        t = lax.rem(place + tiles - slot, tiles)
        at = pl.ds(pl.multiple_of(t * TS, TS), TS + 2 * HALO)
        total = part_ref[slot].astype(F32)
        for step in range(1, group):
            total = total + got_ref[(slot - step) % tiles, step - 1].astype(F32)
        total = (scale * total).astype(BF16)
        rows_back = dot(turn, row_join([total[0], total[1]])).astype(BF16)
        patch = dot(lane_join([rows_back[:rows], rows_back[rows:]]), spread)
        acc_ref[:, at] = acc_ref[:, at] + patch

    lane = lax.broadcasted_iota(jnp.int32, (rows, 2 * HALO), 1)
    low = lane < HALO
    rim_ref[...] = jnp.where(
        low, acc_ref[:, : 2 * HALO], acc_ref[:, width : width + 2 * HALO]
    ).astype(BF16)
    rims = [
        send(rim_ref, left_ref, r_send.at[0], r_recv.at[0], (rank, right)),
        send(rim_ref, right_ref, r_send.at[1], r_recv.at[1], (rank, left)),
    ]
    inner = pltpu.roll(acc_ref[...], width + HALO, 1)[:, :width]
    rims[0].wait_recv()
    rims[1].wait_recv()
    from_left = pltpu.roll(left_ref[...].astype(F32), HALO, 1)
    from_right = pltpu.roll(right_ref[...].astype(F32), HALO, 1)
    from_left = jnp.where(low & (me > 0), from_left, 0.0)
    from_right = jnp.where((lane >= HALO) & (me < line - 1), from_right, 0.0)
    blocks = [
        inner[:, : 2 * HALO] + from_left,
        inner[:, 2 * HALO : width - 2 * HALO],
        inner[:, width - 2 * HALO :] + from_right,
    ]
    out_ref[1] = lane_join(blocks).astype(BF16)
    for copy in halo_copies + spectrum_copies + kernel_copies + [c for copies in grad_copies for c in copies] + rims:
        copy.wait_send()


def on_device(mask, target, start_block, zernike, source_points, source_weight, tile_slit):
    tiles = tile_slit.shape[0]
    rows = mask.shape[0]
    group, line = lax.axis_size("src"), lax.axis_size("tile")
    scale = 1.0 / math.sqrt(TS * (TS + 2 * HALO))
    turns, backs, inverse, adjoint, spread = imaging_tables(group)
    cosine, sine = dft_tables()
    held = [
        jnp.asarray(t)
        for t in (zernike_table(), cosine, sine, start_block, backs, spread, turns, inverse, adjoint)
    ]
    vmem = pl.BlockSpec(memory_space=pltpu.VMEM)
    smem = pl.BlockSpec(memory_space=pltpu.SMEM)
    hbm = pl.BlockSpec(memory_space=pl.ANY)
    dma = pltpu.SemaphoreType.DMA
    own = [x.shape[1:] if x.shape[0] == group and x.ndim == 3 else x.shape for x in held]
    steps = group - 1
    scratch = [pltpu.VMEM(shape, F32) for shape in own]
    scratch += [
        pltpu.VMEM(shape, BF16)
        for shape in [(2 * KB, 2 * KB), (2 * KB, 2 * KB), (KB, 2 * KB), (2 * KB, KB)]
    ]
    scratch += [
        pltpu.VMEM(shape, F32)
        for shape in [(NR * LP, KB), (NR * LP, KB), (KB, KB), (KB, KB), (KB, KB), (NR, 2 * KB)]
    ]
    scratch += [
        pltpu.VMEM((tiles, NR, KB, 2 * KB), BF16),
        pltpu.VMEM((NR * rows, TS), BF16),
        pltpu.VMEM((NR * rows, TS), F32),
        pltpu.VMEM((tiles, 2, KB, KB), BF16),
        pltpu.VMEM((tiles, steps, 2, KB, KB), BF16),
        pltpu.VMEM((tiles, 2, KB, KB), BF16),
        pltpu.VMEM((steps, tiles, 2, KB, KB), BF16),
        pltpu.VMEM((rows, tiles * TS + 2 * HALO), F32),
    ]
    scratch += [pltpu.VMEM((rows, 2 * HALO), BF16)] * 5
    scratch += [
        dma((len(held),)), dma((tiles, NR // GROUP)), dma((tiles, NR // GROUP)),
        dma((tiles, steps)), dma((tiles, steps)), dma((steps,)), dma((steps,)),
        dma((2,)), dma((2,)), dma((2,)), dma((2,)),
    ]
    out = pl.pallas_call(
        functools.partial(
            whole_kernel, group=group, line=line, tiles=tiles, rows=rows, scale=scale
        ),
        out_shape=jax.ShapeDtypeStruct((2,) + target.shape, BF16),
        in_specs=[smem, smem] + [vmem] * 4 + [hbm] * len(held),
        out_specs=vmem,
        scratch_shapes=scratch,
        compiler_params=pltpu.CompilerParams(
            vmem_limit_bytes=56 * 2**20, collective_id=0, has_side_effects=True
        ),
        cost_estimate=pl.CostEstimate(
            flops=8 * 10**9, bytes_accessed=8 * 10**6, transcendentals=0
        ),
    )(tile_slit, zernike, source_points.T, source_weight[None, :], mask, target, *held)
    return out[0], out[1]


def solution(mesh):
    placed = (P("src", "tile"), P("src", "tile"), P(), P(), P(), P(), P("tile"))
    return jax.shard_map(
        on_device,
        mesh=mesh,
        in_specs=placed,
        out_specs=(P("src", "tile"), P("src", "tile")),
        check_vma=False,
    )
```
